256 devices in a mesh: rep: 8 (over y, x_lo), own: 32 (over z, x_hi, core).
Axes of the slice: x: 4 (x_hi: 2, x_lo: 2; x = x_hi * 2 + x_lo), y: 4, z: 8, core: 2. Of those that a mesh axis runs over, the one named last changes fastest.
Arguments:
- act_wide: bfloat16 [1024, 14, 14, 1024], P(('rep', 'own')), may hold values from -6 to 6
- act_middle: bfloat16 [1024, 14, 14, 256], P(('rep', 'own')), may hold values from -6 to 6
- act_narrow: bfloat16 [1024, 14, 14, 256], P(('rep', 'own')), may hold values from -6 to 6
- grad_first: bfloat16 [1024, 14, 14, 256], P(('rep', 'own')), may hold values from -6 to 6
- grad_second: bfloat16 [1024, 14, 14, 256], P(('rep', 'own')), may hold values from -6 to 6
- grad_third: bfloat16 [1024, 14, 14, 1024], P(('rep', 'own')), may hold values from -6 to 6
Outputs:
- update_first: bfloat16 [1024, 256], replicated
- update_second: bfloat16 [2304, 256], replicated
- update_third: bfloat16 [256, 1024], replicated
The draws below stay inside these ranges and needn't reach their ends.
All inputs are finite; a program needn't handle non-finite values. Where the reference program divides by a largest or mean magnitude, that divisor is 1e-20 or more.
Results may differ from the reference program's by a relative error of at most 0.0013.
Values may be sent and summed in bfloat16 or wider, within the bound.
No kernel may reach another device: no remote copies, remote signals or barrier semaphores. Data moves between devices by JAX's collectives and lax.ppermute only.
A program may use at most 128 MiB of HBM per device.

```python
import jax
import jax.numpy as jnp
from jax import lax

WIDE = 1024
MID = 256
HW = 14
NS_ITERS = 6
IMAGES = 1024


def levels(stream_key, extent, split, least, high):
    loudness, own = 1.0, jax.random.fold_in(stream_key, 6)
    for axis_at, blocks in split:
        steps = jnp.exp(jax.random.uniform(jax.random.fold_in(own, axis_at), (blocks,), jnp.float32, least / len(split), high / len(split)))
        loudness = loudness * jnp.repeat(steps, extent[axis_at] // blocks).reshape([-1 if axis == axis_at else 1 for axis in range(len(extent))])
    return loudness


def scatter_about(stream_key, extent, spread, most, shards=(), kind=jnp.bfloat16):
    array = jax.random.normal(stream_key, extent, jnp.float32) * spread
    if len(shards) > 0:
        array = levels(stream_key, extent, shards, -0.22, 0.18) * array
    return jnp.clip(array, min=-most, max=most).astype(kind)


def setup_inputs(seed: int = 0) -> dict:
    keys = jax.random.split(jax.random.key(seed), 7)
    return {
        "act_wide": scatter_about(keys[0], (IMAGES, HW, HW, WIDE), 1.0, 6.0, ((0, 256),)),
        "act_middle": scatter_about(keys[1], (IMAGES, HW, HW, MID), 1.0, 6.0, ((0, 256),)),
        "act_narrow": scatter_about(keys[2], (IMAGES, HW, HW, MID), 1.0, 6.0, ((0, 256),)),
        "grad_first": scatter_about(keys[3], (IMAGES, HW, HW, MID), 1.0, 6.0, ((0, 256),)),
        "grad_second": scatter_about(keys[4], (IMAGES, HW, HW, MID), 1.0, 6.0, ((0, 256),)),
        "grad_third": scatter_about(keys[5], (IMAGES, HW, HW, WIDE), 1.0, 6.0, ((0, 256),)),
    }


damping = 0.1


def invert(gram, count):
    size = gram.shape[-1]
    matrix = gram / count
    identity = jnp.eye(size, dtype=jnp.float32)
    level = jnp.trace(matrix, axis1=-2, axis2=-1) / size
    matrix = matrix + damping * level[..., None, None] * identity
    bound = jnp.max(jnp.sum(jnp.abs(matrix), axis=-1), axis=-1)
    result = identity / bound[..., None, None]
    for step in range(NS_ITERS):
        inner = jnp.matmul(matrix, result, precision=lax.Precision.HIGHEST)
        result = jnp.matmul(result, 2.0 * identity - inner, precision=lax.Precision.HIGHEST)
    return result


def gram_of(left, right):
    return jnp.dot(left.T, right, preferred_element_type=jnp.float32)


def reference(act_wide, act_middle, act_narrow, grad_first, grad_second, grad_third):
    count = float(IMAGES * HW * HW)
    parts = WIDE // MID
    first_in = act_wide.reshape(-1, WIDE)
    third_in = act_narrow.reshape(-1, MID)
    first_out = grad_first.reshape(-1, MID)
    second_out = grad_second.reshape(-1, MID)
    third_out = grad_third.reshape(-1, WIDE)
    padded = jnp.pad(act_middle, ((0, 0), (1, 1), (1, 1), (0, 0)))
    inv_first = invert(gram_of(first_out, first_out), count)
    inv_second = invert(gram_of(second_out, second_out), count)
    inv_third = invert(gram_of(third_in, third_in), count)
    blocks_first = []
    for k in range(parts):
        column = first_in[:, k * MID:(k + 1) * MID]
        left = invert(gram_of(column, column), count)
        tile = gram_of(column, first_out) / count
        inner = jnp.matmul(left, tile, precision=lax.Precision.HIGHEST)
        blocks_first.append(jnp.matmul(inner, inv_first, precision=lax.Precision.HIGHEST).astype(jnp.bfloat16))
    blocks_second = []
    for dy in range(3):
        for dx in range(3):
            patch = padded[:, dy:dy + HW, dx:dx + HW, :].reshape(-1, MID)
            left = invert(gram_of(patch, patch), count)
            tile = gram_of(patch, second_out) / count
            inner = jnp.matmul(left, tile, precision=lax.Precision.HIGHEST)
            blocks_second.append(jnp.matmul(inner, inv_second, precision=lax.Precision.HIGHEST).astype(jnp.bfloat16))
    blocks_third = []
    for j in range(parts):
        column = third_out[:, j * MID:(j + 1) * MID]
        right = invert(gram_of(column, column), count)
        tile = gram_of(third_in, column) / count
        inner = jnp.matmul(inv_third, tile, precision=lax.Precision.HIGHEST)
        blocks_third.append(jnp.matmul(inner, right, precision=lax.Precision.HIGHEST).astype(jnp.bfloat16))
    update_first = jnp.concatenate(blocks_first, axis=0)
    update_second = jnp.concatenate(blocks_second, axis=0)
    update_third = jnp.concatenate(blocks_third, axis=1)
    return (update_first, update_second, update_third)
```

```python
import functools

import jax
import jax.numpy as jnp
from jax import lax
from jax.experimental import pallas as pl
from jax.experimental.pallas import tpu as pltpu
from jax.sharding import PartitionSpec as P

NS_ITERS = 6
DAMPING = 0.1
MID = 256
HALF = 128
SETS = 4
F32 = jnp.float32
BF16 = jnp.bfloat16

REC = (104, 96, 96, 96)
SHARED = (40, 32, 32, 32)
ORDER = tuple(tuple((3 - s - k) % 4 for k in range(4)) for s in range(SETS))
LEAF = tuple(REC[s] + SHARED[s] for s in range(SETS))
LEAF_AT = tuple(sum(LEAF[:s]) for s in range(SETS + 1))


def slot(s, q):
    return sum(((q >> ORDER[s][k]) & 1) << (3 - k) for k in range(4))


def part_rows(s):
    return (8 * REC[s] + 2 * SHARED[s], 9 * REC[s] + SHARED[s])


def dot_t(a, b):
    return lax.dot_general(a, b, (((0,), (0,)), ((), ())), preferred_element_type=F32)


def iotas(n=HALF):
    return lax.broadcasted_iota(jnp.int32, (n, n), 0), lax.broadcasted_iota(jnp.int32, (n, n), 1)


def put(side, keep, send, at, low, high):
    n = low.shape[0]
    keep[at : at + n, :] = jnp.where(side, high, low)
    send[at : at + n, :] = jnp.where(side, low, high)


def put_gram(side, keep, send, at, gram):
    r, c = iotas()
    a, b, d = gram[:HALF, :HALF], gram[:HALF, HALF:], gram[HALF:, HALF:]
    fold = jnp.where(r <= c, a, d)
    for s in range(SETS):
        put(side, keep, send, at[s], fold[32 * s : 32 * s + 32], b[32 * s : 32 * s + 32])
    diag = jnp.broadcast_to(jnp.sum(jnp.where(r == c, d, 0.0), axis=0, keepdims=True), (8, HALF))
    put(side, keep, send, at[0] + 32, diag, diag)


def put_tile(side, keep, send, at, tile):
    for s in range(SETS):
        rows = tile[64 * s : 64 * s + 64]
        put(side, keep, send, at[s], rows[:, :HALF], rows[:, HALF:])


def part_at(part, s, index):
    return sum(part_rows(t)[part] for t in range(s)) + index * REC[s]


def widen(ref, pad):
    images, h, w, c = ref.shape
    pad[:, :w, :] = ref[...].reshape(images * h, w, c)
    pad[:, w:, :] = jnp.zeros((images * h, 16 - w, c), BF16)


def ends_kernel(bits, aw, an, g1, g3, keep, send, pw, pn, p1, p3):
    side = bits[0] == 1
    for ref, pad in ((aw, pw), (an, pn), (g1, p1), (g3, p3)):
        widen(ref, pad)
    rows = pw.shape[0] * 16

    def block(pad, k):
        return pad[:, :, MID * k : MID * k + MID].reshape(rows, MID)

    first_out, third_in = block(p1, 0), block(pn, 0)
    for q in range(8):
        at = [part_at(0, s, q) for s in range(SETS)]
        if q < 4:
            own = block(pw, q)
            tile = dot_t(own, first_out)
        else:
            own = block(p3, q - 4)
            tile = dot_t(third_in, own)
        put_tile(side, keep, send, at, tile)
        put_gram(side, keep, send, [x + 64 for x in at], dot_t(own, own))
    for i, own in enumerate((first_out, third_in)):
        at = [part_at(0, s, 8) + i * SHARED[s] for s in range(SETS)]
        put_gram(side, keep, send, at, dot_t(own, own))


def patch_kernel(bits, am, g2, keep, send, shifted, grads):
    side = bits[0] == 1
    images, h, w, c = am.shape
    shifted[1, :, :, :] = jnp.zeros(shifted.shape[1:], BF16)
    for n in range(images):
        shifted[1, 1 + n * (h + 1) : 1 + n * (h + 1) + h, :w, :] = am[n]
    whole = shifted[1].astype(F32)
    lines = whole.shape[0]
    j = lax.broadcasted_iota(jnp.int32, (lines, 16, c), 1)
    shifted[0] = jnp.where(j < w, pltpu.roll(whole, 1, 1), 0.0).astype(BF16)
    shifted[2] = jnp.where(j < w, pltpu.roll(whole, 15, 1), 0.0).astype(BF16)
    grads[...] = jnp.zeros(grads.shape, BF16)
    for n in range(images):
        grads[n * (h + 1) : n * (h + 1) + h, :w, :] = g2[n]
    span = grads.shape[0]
    second_out = grads[...].reshape(span * 16, c)
    for dx in range(3):
        def picked(lo, hi):
            parts = [shifted[dx, 1 + n * (h + 1) + lo : 1 + n * (h + 1) + hi] for n in range(images)]
            return jnp.concatenate(parts, axis=0).reshape(images * (hi - lo) * 16, c)

        top, inner, bottom = (picked(lo, hi) for lo, hi in ((0, 1), (1, h - 1), (h - 1, h)))
        inner = dot_t(inner, inner)
        top = dot_t(top, top)
        bottom = dot_t(bottom, bottom)
        for dy in range(3):
            q = 3 * dy + dx
            at = [part_at(1, s, q) for s in range(SETS)]
            patch = shifted[dx, dy : dy + span].reshape(span * 16, c)
            put_tile(side, keep, send, at, dot_t(patch, second_out))
            gram = inner
            if dy < 2:
                gram = gram + top
            if dy > 0:
                gram = gram + bottom
            put_gram(side, keep, send, [x + 64 for x in at], gram)
    at = [part_at(1, s, 9) for s in range(SETS)]
    put_gram(side, keep, send, at, dot_t(second_out, second_out))


def held_rows(s, tiles):
    return (tiles + 1) * REC[s] + 3 * SHARED[s]


def first_split_kernel(bits, keep0, got0, keep1, got1, *outs):
    for s in range(SETS):
        keep, send = outs[2 * s], outs[2 * s + 1]
        side = bits[1 + ORDER[s][0]] == 1
        n = REC[s]

        def summed(q):
            part, mine, got = (0, keep0, got0) if q < 8 else (1, keep1, got1)
            at = part_at(part, s, q % 8)
            return mine[at : at + n, :] + got[at : at + n, :]

        for q in range(16):
            if (q >> ORDER[s][0]) & 1:
                continue
            low, high = summed(q), summed(q | 1 << ORDER[s][0])
            put(side, keep, send, slot(s, q) * n, low, high)
        at = 8 * n
        shared = SHARED[s]
        for part, mine, got, i, size in (
            (1, keep1, got1, 8, n),
            (0, keep0, got0, 8, 2 * shared),
            (1, keep1, got1, 9, shared),
        ):
            src = part_at(part, s, i)
            value = mine[src : src + size, :] + got[src : src + size, :]
            keep[at : at + size, :] = value
            send[at : at + size, :] = value
            at += size


def split_kernel(step, bits, *refs):
    tiles = 16 >> step
    for s in range(SETS):
        mine, got = refs[2 * s], refs[2 * s + 1]
        keep, send = refs[2 * SETS + 2 * s], refs[2 * SETS + 2 * s + 1]
        size = (tiles // 2) * REC[s]
        bit = bits[1 + ORDER[s][step]]
        here = pl.ds(pl.multiple_of(bit * size, 8), size)
        there = pl.ds(pl.multiple_of((1 - bit) * size, 8), size)
        keep[:size, :] = mine[here, :] + got[here, :]
        send[:size, :] = mine[there, :] + got[there, :]
        value = mine[2 * size :, :] + got[2 * size :, :]
        keep[size:, :] = value
        send[size:, :] = value


def leaf_kernel(bits, *refs):
    kind = bits[6]
    side = bits[5] == 1
    keep, send = refs[2 * SETS], refs[2 * SETS + 1]
    for s in range(SETS):
        mine, got = refs[2 * s], refs[2 * s + 1]
        n, shared = REC[s], SHARED[s]
        at = LEAF_AT[s]
        put(side, keep, send, at, mine[:n, :] + got[:n, :], mine[n : 2 * n, :] + got[n : 2 * n, :])
        chosen = pl.ds(pl.multiple_of(2 * n + kind * shared, 8), shared)
        last = slice(2 * n + 2 * shared, 2 * n + 3 * shared)
        put(side, keep, send, at + n, mine[chosen, :] + got[chosen, :], mine[last, :] + got[last, :])


def mm(a, b):
    return jnp.dot(a, b, precision=lax.Precision.HIGHEST, preferred_element_type=F32)


def unfold(fold, b, diag):
    r, c = iotas()
    turned = fold.T
    a = jnp.where(r <= c, fold, turned)
    d = jnp.where(r > c, fold, jnp.where(r < c, turned, jnp.broadcast_to(diag, fold.shape)))
    top = jnp.concatenate([a, b], axis=1)
    return jnp.concatenate([top, jnp.concatenate([b.T, d], axis=1)], axis=0)


def residual(gram, count):
    r, c = iotas(MID)
    matrix = gram / count
    level = jnp.sum(jnp.where(r == c, matrix, 0.0)) / MID
    matrix = matrix + jnp.where(r == c, DAMPING * level, 0.0)
    bound = jnp.max(jnp.sum(jnp.abs(matrix), axis=0, keepdims=True))
    return jnp.where(r == c, 1.0, 0.0) - matrix / bound, bound


def solve_kernel(count, bits, mine, mate, out):
    side = bits[0] == 1
    low = jnp.where(side, mate[...], mine[...])
    high = jnp.where(side, mine[...], mate[...])

    def gather(part, offset, rows):
        return jnp.concatenate([part[LEAF_AT[s] + offset(s) : LEAF_AT[s] + offset(s) + rows] for s in range(SETS)], axis=0)

    def gram(offset):
        at = offset(0) + 32
        return unfold(gather(low, offset, 32), gather(high, offset, 32), low[at : at + 1])

    zero = lambda s: 0
    tile = jnp.concatenate([gather(low, zero, 64), gather(high, zero, 64)], axis=1) / count
    own, own_bound = residual(gram(lambda s: 64), count)
    shared, shared_bound = residual(gram(lambda s: REC[s]), count)
    third = bits[7] == 1
    left, right = jnp.where(third, shared, own), jnp.where(third, own, shared)
    r, c = iotas(MID)
    product = jnp.where(r == c, 1.0, 0.0) + right
    tile = tile + mm(left, tile)
    for step in range(1, NS_ITERS):
        left, right = mm(left, left), mm(right, right)
        tile = tile + mm(left, tile)
        product = product + mm(product, right)
    result = mm(tile / own_bound, product / shared_bound)
    out[...] = result.astype(BF16)


def join_kernel(*refs):
    n = len(refs) // 3
    for i in range(n):
        a, b, out = refs[2 * i], refs[2 * i + 1], refs[2 * n + i]
        k = a.shape[0]
        out[:k] = a[...]
        out[k:] = b[...]


def place_kernel(bits, *refs):
    out1, out2, out3 = refs[-3:]
    lows, highs = refs[0 : 2 * SETS], refs[2 * SETS : 4 * SETS]
    last_low, last_high = refs[4 * SETS], refs[4 * SETS + 1]
    own = bits[8]
    side = bits[0] == 1
    for half in range(2):
        swap = side if half == 0 else jnp.logical_not(side)
        for s in range(SETS):
            order = ORDER[s]
            for q in range(16):
                other = jnp.bitwise_xor(own, q)
                index = sum(((other >> order[k]) & 1) << k for k in range(3))
                late = ((other >> order[3]) & 1) == 1
                at = half * HALF + 32 * s
                mine = jnp.where(late, lows[2 * s + 1][index], lows[2 * s][index])
                mate = jnp.where(late, highs[2 * s + 1][index], highs[2 * s][index])
                value = jnp.where(swap, mate, mine)
                if q < 4:
                    out1[q * MID + at : q * MID + at + 32, :] = value
                elif q < 8:
                    out3[at : at + 32, (q - 4) * MID : (q - 3) * MID] = value
                else:
                    out2[(q - 8) * MID + at : (q - 8) * MID + at + 32, :] = value
        value = jnp.where(swap, last_high[...], last_low[...])
        out2[8 * MID + half * HALF : 8 * MID + half * HALF + HALF, :] = value


VMEM = pl.BlockSpec(memory_space=pltpu.VMEM)
SMEM = pl.BlockSpec(memory_space=pltpu.SMEM)


def call(kernel, bits, args, outs, scratch=(), flops=0):
    size = sum(a.size * a.dtype.itemsize for a in args) + sum(o.size * o.dtype.itemsize for o in outs)
    many = len(outs) > 1
    return pl.pallas_call(
        kernel,
        out_shape=tuple(outs) if many else outs[0],
        in_specs=[SMEM] + [VMEM] * len(args),
        out_specs=tuple([VMEM] * len(outs)) if many else VMEM,
        scratch_shapes=list(scratch),
        compiler_params=pltpu.CompilerParams(vmem_limit_bytes=48 * 2**20),
        cost_estimate=pl.CostEstimate(flops=flops, bytes_accessed=size, transcendentals=0),
    )(bits, *args)


AXES = ("rep", "own")


def place_of(device):
    rep, own = divmod(device, 32)
    return rep // 2, (own // 2) % 2 * 2 + rep % 2, own // 4, own % 2


def device_of(y, x, z, c):
    return (y * 2 + x % 2) * 32 + z * 4 + x // 2 * 2 + c


def route(move):
    return [(d, device_of(*move(*place_of(d)))) for d in range(256)]


ROUTE_C = route(lambda y, x, z, c: (y, x, z, 1 - c))
ROUTE_XY = {
    3: route(lambda y, x, z, c: (y, x ^ 1, z, c)),
    2: route(lambda y, x, z, c: (y, 3 - x, z, c)),
    1: route(lambda y, x, z, c: (y ^ 1, x, z, c)),
    0: route(lambda y, x, z, c: (3 - y, x, z, c)),
}
ROUTE_Z1 = route(lambda y, x, z, c: (y, x, z ^ 1, c))
ROUTE_Z2 = route(lambda y, x, z, c: (y, x, z ^ 3, c))
ROUTE_Z3 = route(lambda y, x, z, c: (y, x, 7 - z, c))


def send_to(value, way):
    return lax.ppermute(value, AXES, way)


def on_device(act_wide, act_middle, act_narrow, grad_first, grad_second, grad_third):
    images, height, width, wide = act_wide.shape
    middle = act_middle.shape[3]
    count = float(images * height * width * 256)
    rep, own = lax.axis_index("rep"), lax.axis_index("own")
    core, x, z, y = own & 1, (own >> 1 & 1) * 2 + (rep & 1), own >> 2, rep >> 1
    bit3, bit2 = (x ^ (x >> 1)) & 1, x >> 1
    bit1, bit0 = (y ^ (y >> 1)) & 1, y >> 1
    q = bit3 * 8 + bit2 * 4 + bit1 * 2 + bit0
    odd = ((z + 1) >> 1) & 1
    kind = jnp.where(q < 4, 0, jnp.where(q < 8, 1, 2))
    third = jnp.where((kind == 1) & (odd == 0), 1, 0)
    bits = jnp.stack([core, bit0, bit1, bit2, bit3, odd, kind, third, q]).astype(jnp.int32)

    lines = images * height
    rows = [sum(part_rows(s)[part] for s in range(SETS)) for part in range(2)]
    made = [jax.ShapeDtypeStruct((n, HALF), F32) for n in rows]
    pads = [pltpu.VMEM((lines, 16, n), BF16) for n in (wide, middle, middle, wide)]
    keep0, send0 = call(
        ends_kernel, bits, (act_wide, act_narrow, grad_first, grad_third), [made[0]] * 2, pads, 2 * 18 * 896 * 65536
    )
    got0 = send_to(send0, ROUTE_C)
    span = images * (height + 1)
    keep1, send1 = call(
        patch_kernel,
        bits,
        (act_middle, grad_second),
        [made[1]] * 2,
        [pltpu.VMEM((3, span + 2, 16, middle), BF16), pltpu.VMEM((span, 16, middle), BF16)],
        2 * 13 * 960 * 65536,
    )
    got1 = send_to(send1, ROUTE_C)

    def pairs(tiles):
        shapes = [jax.ShapeDtypeStruct((held_rows(s, tiles), HALF), F32) for s in range(SETS)]
        return [shape for shape in shapes for _ in range(2)]

    held = call(first_split_kernel, bits, (keep0, got0, keep1, got1), pairs(8))
    for step in range(4):
        args = []
        for s in range(SETS):
            args += [held[2 * s], send_to(held[2 * s + 1], ROUTE_XY[ORDER[s][step]])]
        if step < 3:
            held = call(functools.partial(split_kernel, step + 1), bits, args, pairs(4 >> step))
    leaf = jax.ShapeDtypeStruct((LEAF_AT[-1], HALF), F32)
    keep, send = call(leaf_kernel, bits, args, [leaf] * 2)
    total = keep + send_to(send, ROUTE_Z1)
    cut = LEAF_AT[2]
    one, two = total[:cut], total[cut:]
    one, two = one + send_to(one, ROUTE_Z2), two + send_to(two, ROUTE_Z3)
    one, two = one + send_to(one, ROUTE_Z3), two + send_to(two, ROUTE_Z2)
    total = jnp.concatenate([one, two], axis=0)
    result = call(
        functools.partial(solve_kernel, count),
        bits,
        (total, send_to(total, ROUTE_C)),
        [jax.ShapeDtypeStruct((MID, MID), BF16)],
        flops=2 * 22 * 6 * MID**3,
    )

    mine = lax.dynamic_slice_in_dim(result, core * HALF, HALF, 0)
    other = send_to(mine, ROUTE_Z1)
    tile, last = jnp.where(odd == 0, mine, other), jnp.where(odd == 0, other, mine)
    held = [tile[32 * s : 32 * s + 32][None] for s in range(SETS)]
    for step in range(4):
        got = [send_to(held[s], ROUTE_XY[ORDER[s][step]]) for s in range(SETS)]
        pieces = [a for pair in zip(held, got) for a in pair]
        if step < 3:
            outs = [jax.ShapeDtypeStruct((2 << step, 32, MID), BF16)] * SETS
            held = call(lambda bits, *refs: join_kernel(*refs), bits, pieces, outs)
    pieces = pieces + [send_to(a, ROUTE_C) for a in pieces] + [last, send_to(last, ROUTE_C)]
    outs = [
        jax.ShapeDtypeStruct((wide, middle), BF16),
        jax.ShapeDtypeStruct((9 * middle, middle), BF16),
        jax.ShapeDtypeStruct((middle, wide), BF16),
    ]
    return call(place_kernel, bits, pieces, outs)


def solution(mesh):
    placed = P(("rep", "own"), None, None, None)
    return jax.shard_map(on_device, mesh=mesh, in_specs=(placed,) * 6, out_specs=(P(), P(), P()), check_vma=False)
```

```python
import functools

import jax
import jax.numpy as jnp
from jax import lax
from jax.experimental import pallas as pl
from jax.experimental.pallas import tpu as pltpu
from jax.sharding import Mesh
from jax.sharding import PartitionSpec as P

NS_ITERS = 6
DAMPING = 0.1
MID = 256
HALF = 128
SETS = 2
F32 = jnp.float32
BF16 = jnp.bfloat16

REC = (200, 192)
SHARED = (72, 64)
ORDER = (((3, 2, 1, 0), (1, 0, 3, 2)), ((2, 3, 0, 1), (0, 1, 2, 3)))
LEAF = tuple(REC[s] + SHARED[s] for s in range(SETS))
LEAF_AT = tuple(sum(LEAF[:s]) for s in range(SETS + 1))


def slot(order, q):
    return sum(((q >> order[k]) & 1) << (3 - k) for k in range(4))


def part_rows(s):
    return (8 * REC[s] + 2 * SHARED[s], 9 * REC[s] + SHARED[s])


def dot_t(a, b):
    return lax.dot_general(a, b, (((0,), (0,)), ((), ())), preferred_element_type=F32)


def iotas(n=HALF):
    return lax.broadcasted_iota(jnp.int32, (n, n), 0), lax.broadcasted_iota(jnp.int32, (n, n), 1)


def put(side, keep, send, at, low, high):
    n = low.shape[0]
    keep[at : at + n, :] = jnp.where(side, high, low)
    send[at : at + n, :] = jnp.where(side, low, high)


def put_gram(side, keep, send, at, gram):
    r, c = iotas()
    a, b, d = gram[:HALF, :HALF], gram[:HALF, HALF:], gram[HALF:, HALF:]
    fold = jnp.where(r <= c, a, d)
    for s in range(SETS):
        put(side, keep, send, at[s], fold[64 * s : 64 * s + 64], b[64 * s : 64 * s + 64])
    diag = jnp.broadcast_to(jnp.sum(jnp.where(r == c, d, 0.0), axis=0, keepdims=True), (8, HALF))
    put(side, keep, send, at[0] + 64, diag, diag)


def put_tile(side, keep, send, at, tile):
    for s in range(SETS):
        rows = tile[HALF * s : HALF * s + HALF]
        put(side, keep, send, at[s], rows[:, :HALF], rows[:, HALF:])


def part_at(part, s, index):
    return sum(part_rows(t)[part] for t in range(s)) + index * REC[s]


def widen(ref, pad):
    images, h, w, c = ref.shape
    pad[:, :w, :] = ref[...].reshape(images * h, w, c)
    pad[:, w:, :] = jnp.zeros((images * h, 16 - w, c), BF16)


def ends_kernel(bits, aw, an, g1, g3, keep, send, pw, pn, p1, p3):
    side = bits[0] == 1
    for ref, pad in ((aw, pw), (an, pn), (g1, p1), (g3, p3)):
        widen(ref, pad)
    rows = pw.shape[0] * 16

    def block(pad, k):
        return pad[:, :, MID * k : MID * k + MID].reshape(rows, MID)

    first_out, third_in = block(p1, 0), block(pn, 0)
    for q in range(8):
        at = [part_at(0, s, q) for s in range(SETS)]
        if q < 4:
            own = block(pw, q)
            tile = dot_t(own, first_out)
        else:
            own = block(p3, q - 4)
            tile = dot_t(third_in, own)
        put_tile(side, keep, send, at, tile)
        put_gram(side, keep, send, [x + HALF for x in at], dot_t(own, own))
    for i, own in enumerate((first_out, third_in)):
        at = [part_at(0, s, 8) + i * SHARED[s] for s in range(SETS)]
        put_gram(side, keep, send, at, dot_t(own, own))


def patch_kernel(bits, am, g2, keep, send, shifted, grads):
    side = bits[0] == 1
    images, h, w, c = am.shape
    shifted[1, :, :, :] = jnp.zeros(shifted.shape[1:], BF16)
    for n in range(images):
        shifted[1, 1 + n * (h + 1) : 1 + n * (h + 1) + h, :w, :] = am[n]
    whole = shifted[1].astype(F32)
    lines = whole.shape[0]
    j = lax.broadcasted_iota(jnp.int32, (lines, 16, c), 1)
    shifted[0] = jnp.where(j < w, pltpu.roll(whole, 1, 1), 0.0).astype(BF16)
    shifted[2] = jnp.where(j < w, pltpu.roll(whole, 15, 1), 0.0).astype(BF16)
    grads[...] = jnp.zeros(grads.shape, BF16)
    for n in range(images):
        grads[n * (h + 1) : n * (h + 1) + h, :w, :] = g2[n]
    span = grads.shape[0]
    second_out = grads[...].reshape(span * 16, c)
    for dx in range(3):
        def picked(lo, hi):
            parts = [shifted[dx, 1 + n * (h + 1) + lo : 1 + n * (h + 1) + hi] for n in range(images)]
            return jnp.concatenate(parts, axis=0).reshape(images * (hi - lo) * 16, c)

        top, inner, bottom = (picked(lo, hi) for lo, hi in ((0, 1), (1, h - 1), (h - 1, h)))
        inner = dot_t(inner, inner)
        top = dot_t(top, top)
        bottom = dot_t(bottom, bottom)
        for dy in range(3):
            q = 3 * dy + dx
            at = [part_at(1, s, q) for s in range(SETS)]
            patch = shifted[dx, dy : dy + span].reshape(span * 16, c)
            put_tile(side, keep, send, at, dot_t(patch, second_out))
            gram = inner
            if dy < 2:
                gram = gram + top
            if dy > 0:
                gram = gram + bottom
            put_gram(side, keep, send, [x + HALF for x in at], gram)
    at = [part_at(1, s, 9) for s in range(SETS)]
    put_gram(side, keep, send, at, dot_t(second_out, second_out))


def held_rows(s, tiles):
    return (tiles + 1) * REC[s] + 3 * SHARED[s]


def first_split_kernel(bits, keep0, got0, keep1, got1, *outs):
    for core in range(2):

        @pl.when(bits[0] == core)
        def _(core=core):
            first_split(ORDER[core], bits, keep0, got0, keep1, got1, outs)


def first_split(orders, bits, keep0, got0, keep1, got1, outs):
    for s in range(SETS):
        keep, send = outs[2 * s], outs[2 * s + 1]
        lead = orders[s][0]
        side = bits[1 + lead] == 1
        n = REC[s]

        def summed(q):
            part, mine, got = (0, keep0, got0) if q < 8 else (1, keep1, got1)
            at = part_at(part, s, q % 8)
            return mine[at : at + n, :] + got[at : at + n, :]

        for q in range(16):
            if (q >> lead) & 1:
                continue
            put(side, keep, send, slot(orders[s], q) * n, summed(q), summed(q | 1 << lead))
        at = 8 * n
        shared = SHARED[s]
        for part, mine, got, i, size in (
            (1, keep1, got1, 8, n),
            (0, keep0, got0, 8, 2 * shared),
            (1, keep1, got1, 9, shared),
        ):
            src = part_at(part, s, i)
            value = mine[src : src + size, :] + got[src : src + size, :]
            keep[at : at + size, :] = value
            send[at : at + size, :] = value
            at += size


def split_kernel(step, bits, *refs):
    tiles = 16 >> step
    for s in range(SETS):
        mine, got = refs[2 * s], refs[2 * s + 1]
        keep, send = refs[2 * SETS + 2 * s], refs[2 * SETS + 2 * s + 1]
        size = (tiles // 2) * REC[s]
        bit = bits[9 + 4 * s + step]
        here = pl.ds(pl.multiple_of(bit * size, 8), size)
        there = pl.ds(pl.multiple_of((1 - bit) * size, 8), size)
        keep[:size, :] = mine[here, :] + got[here, :]
        send[:size, :] = mine[there, :] + got[there, :]
        value = mine[2 * size :, :] + got[2 * size :, :]
        keep[size:, :] = value
        send[size:, :] = value


def leaf_kernel(bits, *refs):
    kind = bits[6]
    side = bits[5] == 1
    keep, send = refs[2 * SETS], refs[2 * SETS + 1]
    for s in range(SETS):
        mine, got = refs[2 * s], refs[2 * s + 1]
        n, shared = REC[s], SHARED[s]
        at = LEAF_AT[s]
        put(side, keep, send, at, mine[:n, :] + got[:n, :], mine[n : 2 * n, :] + got[n : 2 * n, :])
        chosen = pl.ds(pl.multiple_of(2 * n + kind * shared, 8), shared)
        last = slice(2 * n + 2 * shared, 2 * n + 3 * shared)
        put(side, keep, send, at + n, mine[chosen, :] + got[chosen, :], mine[last, :] + got[last, :])


def mm(a, b):
    return jnp.dot(a, b, precision=lax.Precision.HIGHEST, preferred_element_type=F32)


def unfold(fold, b, diag):
    r, c = iotas()
    turned = fold.T
    a = jnp.where(r <= c, fold, turned)
    d = jnp.where(r > c, fold, jnp.where(r < c, turned, jnp.broadcast_to(diag, fold.shape)))
    top = jnp.concatenate([a, b], axis=1)
    return jnp.concatenate([top, jnp.concatenate([b.T, d], axis=1)], axis=0)


def residual(gram, count):
    r, c = iotas(MID)
    matrix = gram / count
    level = jnp.sum(jnp.where(r == c, matrix, 0.0)) / MID
    matrix = matrix + jnp.where(r == c, DAMPING * level, 0.0)
    bound = jnp.max(jnp.sum(jnp.abs(matrix), axis=0, keepdims=True))
    return jnp.where(r == c, 1.0, 0.0) - matrix / bound, bound


def solve_kernel(count, bits, mine, mate, out):
    side = bits[0] == 1
    low = jnp.where(side, mate[...], mine[...])
    high = jnp.where(side, mine[...], mate[...])

    def gather(part, offset, rows):
        starts = [LEAF_AT[s] + offset(s) for s in range(SETS)]
        return jnp.concatenate([part[at : at + rows] for at in starts], axis=0)

    def gram(offset):
        at = offset(0) + 64
        return unfold(gather(low, offset, 64), gather(high, offset, 64), low[at : at + 1])

    zero = lambda s: 0
    tile = jnp.concatenate([gather(low, zero, HALF), gather(high, zero, HALF)], axis=1) / count
    own, own_bound = residual(gram(lambda s: HALF), count)
    shared, shared_bound = residual(gram(lambda s: REC[s]), count)
    third = bits[7] == 1
    left, right = jnp.where(third, shared, own), jnp.where(third, own, shared)
    r, c = iotas(MID)
    product = jnp.where(r == c, 1.0, 0.0) + right
    tile = tile + mm(left, tile)
    for step in range(1, NS_ITERS):
        left, right = mm(left, left), mm(right, right)
        tile = tile + mm(left, tile)
        product = product + mm(product, right)
    result = mm(tile / own_bound, product / shared_bound)
    out[...] = jnp.where(side, result[HALF:], result[:HALF]).astype(BF16)


def place_kernel(bits, mine, mate, last, last_mate, out1, out2, out3):
    side = bits[0] == 1
    for half in range(2):
        swap = side if half == 0 else jnp.logical_not(side)
        at = half * HALF
        for j in range(16):
            value = jnp.where(swap, mate[j], mine[j])
            q = tile_of(j // 4, j % 2 * 2 + j // 2 % 2)
            if q < 4:
                out1[q * MID + at : q * MID + at + HALF, :] = value
            elif q < 8:
                out3[at : at + HALF, (q - 4) * MID : (q - 3) * MID] = value
            else:
                out2[(q - 8) * MID + at : (q - 8) * MID + at + HALF, :] = value
        out2[8 * MID + at : 8 * MID + at + HALF, :] = jnp.where(swap, last_mate[...], last[...])


VMEM = pl.BlockSpec(memory_space=pltpu.VMEM)
SMEM = pl.BlockSpec(memory_space=pltpu.SMEM)


def scratch_arrays(scratch):
    return [jax.ShapeDtypeStruct(a.shape, a.dtype) for a in scratch]


def call(kernel, bits, args, outs, scratch=(), flops=0, room=4):
    size = sum(a.size * a.dtype.itemsize for a in args) + sum(o.size * o.dtype.itemsize for o in outs)
    held = sum(a.size * a.dtype.itemsize for a in scratch_arrays(scratch))
    many = len(outs) > 1
    return pl.pallas_call(
        kernel,
        out_shape=tuple(outs) if many else outs[0],
        in_specs=[SMEM] + [VMEM] * len(args),
        out_specs=tuple([VMEM] * len(outs)) if many else VMEM,
        scratch_shapes=list(scratch),
        compiler_params=pltpu.CompilerParams(vmem_limit_bytes=size * 5 // 4 + held + room * 2**20),
        cost_estimate=pl.CostEstimate(flops=flops, bytes_accessed=size, transcendentals=0),
    )(bits, *args)


AXES = ("y", "x_lo", "z", "x_hi", "core")
SIZES = (4, 2, 8, 2, 2)


def place_of(device):
    rep, own = divmod(device, 32)
    return rep // 2, (own // 2) % 2 * 2 + rep % 2, own // 4, own % 2


def device_of(y, x, z, c):
    return (y * 2 + x % 2) * 32 + z * 4 + x // 2 * 2 + c


def route(move):
    return [(d, device_of(*move(*place_of(d)))) for d in range(256)]


ROUTE_C = route(lambda y, x, z, c: (y, x, z, 1 - c))
MOVE = {
    3: lambda y, x, z, c: (y, x ^ 1, z, c),
    2: lambda y, x, z, c: (y, 3 - x, z, c),
    1: lambda y, x, z, c: (y ^ 1, x, z, c),
    0: lambda y, x, z, c: (3 - y, x, z, c),
}
ROUTE_XY = [
    [route(lambda y, x, z, c: MOVE[ORDER[c][s][step]](y, x, z, c)) for step in range(4)] for s in range(SETS)
]
ROUTE_Z1 = route(lambda y, x, z, c: (y, x, z ^ 1, c))
ROUTE_Z2 = route(lambda y, x, z, c: (y, x, 7 - z if c else z ^ 3, c))
ROUTE_Z3 = route(lambda y, x, z, c: (y, x, z ^ 3 if c else 7 - z, c))


def tile_of(y, x):
    return ((x ^ (x >> 1)) & 1) * 8 + (x >> 1) * 4 + ((y ^ (y >> 1)) & 1) * 2 + (y >> 1)


def send_to(value, way):
    return lax.ppermute(value, AXES, way)


def on_device(act_wide, act_middle, act_narrow, grad_first, grad_second, grad_third):
    images, height, width, wide = act_wide.shape
    middle = act_middle.shape[3]
    count = float(images * height * width * 256)
    y, z, core = lax.axis_index("y"), lax.axis_index("z"), lax.axis_index("core")
    x = lax.axis_index("x_hi") * 2 + lax.axis_index("x_lo")
    q = tile_of(y, x)
    own = [(q >> i) & 1 for i in range(4)]
    turns = [jnp.where(core == 1, own[ORDER[1][s][k]], own[ORDER[0][s][k]]) for s in range(SETS) for k in range(4)]
    odd = ((z + 1) >> 1) & 1
    kind = jnp.where(q < 4, 0, jnp.where(q < 8, 1, 2))
    third = jnp.where((kind == 1) & (odd == 0), 1, 0)
    bits = jnp.stack([core, *own, odd, kind, third, q, *turns]).astype(jnp.int32)

    lines = images * height
    rows = [sum(part_rows(s)[part] for s in range(SETS)) for part in range(2)]
    made = [jax.ShapeDtypeStruct((n, HALF), F32) for n in rows]
    pads = [pltpu.VMEM((lines, 16, n), BF16) for n in (wide, middle, middle, wide)]
    keep0, send0 = call(
        ends_kernel, bits, (act_wide, act_narrow, grad_first, grad_third), [made[0]] * 2, pads, 2 * 18 * 896 * 65536
    )
    got0 = send_to(send0, ROUTE_C)
    span = images * (height + 1)
    keep1, send1 = call(
        patch_kernel,
        bits,
        (act_middle, grad_second),
        [made[1]] * 2,
        [pltpu.VMEM((3, span + 2, 16, middle), BF16), pltpu.VMEM((span, 16, middle), BF16)],
        2 * 13 * 960 * 65536,
    )
    got1 = send_to(send1, ROUTE_C)

    def pairs(tiles):
        shapes = [jax.ShapeDtypeStruct((held_rows(s, tiles), HALF), F32) for s in range(SETS)]
        return [shape for shape in shapes for _ in range(2)]

    held = call(first_split_kernel, bits, (keep0, got0, keep1, got1), pairs(8))
    for step in range(4):
        args = []
        for s in range(SETS):
            args += [held[2 * s], send_to(held[2 * s + 1], ROUTE_XY[s][step])]
        if step < 3:
            held = call(functools.partial(split_kernel, step + 1), bits, args, pairs(4 >> step))
    leaf = jax.ShapeDtypeStruct((LEAF_AT[-1], HALF), F32)
    keep, send = call(leaf_kernel, bits, args, [leaf] * 2)
    total = keep + send_to(send, ROUTE_Z1)
    total = total + send_to(total, ROUTE_Z2)
    total = total + send_to(total, ROUTE_Z3)
    mine = call(
        functools.partial(solve_kernel, count),
        bits,
        (total, send_to(total, ROUTE_C)),
        [jax.ShapeDtypeStruct((HALF, MID), BF16)],
        flops=2 * 22 * 6 * MID**3,
        room=24,
    )

    other = send_to(mine, ROUTE_Z1)
    tile, last = jnp.where(odd == 0, mine, other), jnp.where(odd == 0, other, mine)
    tiles = jnp.broadcast_to(tile[None], (16, HALF, MID))
    tiles = lax.all_to_all(tiles, ("y", "x_lo", "x_hi"), 0, 0)
    pieces = (tiles, send_to(tiles, ROUTE_C), last, send_to(last, ROUTE_C))
    outs = [
        jax.ShapeDtypeStruct((wide, middle), BF16),
        jax.ShapeDtypeStruct((9 * middle, middle), BF16),
        jax.ShapeDtypeStruct((middle, wide), BF16),
    ]
    return call(place_kernel, bits, pieces, outs)


def solution(mesh):
    mesh = Mesh(mesh.devices.reshape(SIZES), AXES)
    placed = P(AXES, None, None, None)
    return jax.shard_map(on_device, mesh=mesh, in_specs=(placed,) * 6, out_specs=(P(), P(), P()), check_vma=False)
```

```python
import functools

import jax
import jax.numpy as jnp
from jax import lax
from jax.experimental import pallas as pl
from jax.experimental.pallas import tpu as pltpu
from jax.sharding import Mesh
from jax.sharding import PartitionSpec as P

NS_ITERS = 6
DAMPING = 0.1
MID = 256
HALF = 128
SETS = 2
F32 = jnp.float32
BF16 = jnp.bfloat16

GRAM = (72, 64)
TILE = (128, 128)
ORDER = (((3, 2, 1, 0), (1, 0, 3, 2)), ((2, 3, 0, 1), (0, 1, 2, 3)))
def slot(order, q):
    return sum(((q >> order[k]) & 1) << (3 - k) for k in range(4))


def dot_t(a, b):
    return lax.dot_general(a, b, (((0,), (0,)), ((), ())), preferred_element_type=F32)


def iotas(n=HALF):
    return lax.broadcasted_iota(jnp.int32, (n, n), 0), lax.broadcasted_iota(jnp.int32, (n, n), 1)


def put(side, keep, send, at, low, high):
    n = low.shape[0]
    keep[at : at + n, :] = jnp.where(side, high, low)
    send[at : at + n, :] = jnp.where(side, low, high)


def put_gram(side, keep, send, many, i, gram):
    r, c = iotas()
    a, b, d = gram[:HALF, :HALF], gram[:HALF, HALF:], gram[HALF:, HALF:]
    fold = jnp.where(r <= c, a, d)
    for s in range(SETS):
        at = many * sum(GRAM[:s]) + i * GRAM[s]
        put(side, keep, send, at, fold[64 * s : 64 * s + 64], b[64 * s : 64 * s + 64])
    diag = jnp.broadcast_to(jnp.sum(jnp.where(r == c, d, 0.0), axis=0, keepdims=True), (8, HALF))
    put(side, keep, send, i * GRAM[0] + 64, diag, diag)


def put_tile(side, keep, send, many, i, tile):
    for s in range(SETS):
        rows = tile[HALF * s : HALF * s + HALF]
        put(side, keep, send, many * sum(TILE[:s]) + i * TILE[s], rows[:, :HALF], rows[:, HALF:])


def widen(ref, pad):
    images, h, w, c = ref.shape
    pad[:, :w, :] = ref[...].reshape(images * h, w, c)
    pad[:, w:, :] = jnp.zeros((images * h, 16 - w, c), BF16)


def columns(pad, k):
    return pad[:, :, MID * k : MID * k + MID].reshape(pad.shape[0] * 16, MID)


def end_grams_kernel(bits, aw, an, g1, g3, keep, send, pw, pn, p1, p3):
    side = bits[0] == 1
    for ref, pad in ((aw, pw), (an, pn), (g1, p1), (g3, p3)):
        widen(ref, pad)
    blocks = [(pw, k) for k in range(4)] + [(p3, k) for k in range(4)] + [(p1, 0), (pn, 0)]
    for i, block in enumerate(blocks):
        own = columns(*block)
        put_gram(side, keep, send, 10, i, dot_t(own, own))


def end_tiles_kernel(bits, aw, an, g1, g3, keep, send, pw, pn, p1, p3):
    side = bits[0] == 1
    for ref, pad in ((aw, pw), (an, pn), (g1, p1), (g3, p3)):
        widen(ref, pad)
    first_out, third_in = columns(p1, 0), columns(pn, 0)
    for q in range(8):
        tile = dot_t(columns(pw, q), first_out) if q < 4 else dot_t(third_in, columns(p3, q - 4))
        put_tile(side, keep, send, 8, q, tile)


def shift(am, shifted):
    images, h, w, c = am.shape
    shifted[1, :, :, :] = jnp.zeros(shifted.shape[1:], BF16)
    for n in range(images):
        shifted[1, 1 + n * (h + 1) : 1 + n * (h + 1) + h, :w, :] = am[n]
    whole = shifted[1].astype(F32)
    j = lax.broadcasted_iota(jnp.int32, whole.shape, 1)
    shifted[0] = jnp.where(j < w, pltpu.roll(whole, 1, 1), 0.0).astype(BF16)
    shifted[2] = jnp.where(j < w, pltpu.roll(whole, 15, 1), 0.0).astype(BF16)


def spread(g2, grads):
    images, h, w, c = g2.shape
    grads[...] = jnp.zeros(grads.shape, BF16)
    for n in range(images):
        grads[n * (h + 1) : n * (h + 1) + h, :w, :] = g2[n]
    return grads[...].reshape(grads.shape[0] * 16, c)


def patch_grams_kernel(bits, am, g2, keep, send, shifted, grads):
    side = bits[0] == 1
    images, h, w, c = am.shape
    shift(am, shifted)
    second_out = spread(g2, grads)
    put_gram(side, keep, send, 10, 9, dot_t(second_out, second_out))
    for dx in range(3):
        def picked(lo, hi):
            parts = [shifted[dx, 1 + n * (h + 1) + lo : 1 + n * (h + 1) + hi] for n in range(images)]
            return jnp.concatenate(parts, axis=0).reshape(images * (hi - lo) * 16, c)

        top, inner, bottom = (dot_t(x, x) for x in (picked(0, 1), picked(1, h - 1), picked(h - 1, h)))
        upper = inner + top
        put_gram(side, keep, send, 10, dx, upper)
        put_gram(side, keep, send, 10, 3 + dx, upper + bottom)
        put_gram(side, keep, send, 10, 6 + dx, inner + bottom)


def patch_tiles_kernel(bits, am, g2, keep, send, shifted, grads):
    side = bits[0] == 1
    shift(am, shifted)
    second_out = spread(g2, grads)
    span, c = grads.shape[0], am.shape[3]
    for q in range(9):
        patch = shifted[q % 3, q // 3 : q // 3 + span].reshape(span * 16, c)
        put_tile(side, keep, send, 9, q, dot_t(patch, second_out))


def first_split_kernel(rec, many, extra, bits, keep0, got0, keep1, got1, *outs):
    for core in range(2):

        @pl.when(bits[0] == core)
        def _(core=core):
            first_split(ORDER[core], rec, many, extra, bits, ((keep0, got0), (keep1, got1)), outs)


def first_split(orders, rec, many, extra, bits, parts, outs):
    for s in range(SETS):
        keep, send = outs[2 * s], outs[2 * s + 1]
        lead = orders[s][0]
        side = bits[1 + lead] == 1
        n = rec[s]

        def summed(part, i):
            mine, got = parts[part]
            at = many[part] * sum(rec[:s]) + i * n
            return mine[at : at + n, :] + got[at : at + n, :]

        for q in range(16):
            if (q >> lead) & 1:
                continue
            other = q | 1 << lead
            put(side, keep, send, slot(orders[s], q) * n, summed(q // 8, q % 8), summed(other // 8, other % 8))
        for i, (part, j) in enumerate(extra):
            value = summed(part, j)
            keep[(8 + i) * n : (9 + i) * n, :] = value
            send[(8 + i) * n : (9 + i) * n, :] = value


def split_kernel(rec, step, bits, *refs):
    tiles = 16 >> step
    for s in range(SETS):
        mine, got = refs[2 * s], refs[2 * s + 1]
        keep, send = refs[2 * SETS + 2 * s], refs[2 * SETS + 2 * s + 1]
        size = (tiles // 2) * rec[s]
        bit = bits[9 + 4 * s + step]
        here = pl.ds(pl.multiple_of(bit * size, 8), size)
        there = pl.ds(pl.multiple_of((1 - bit) * size, 8), size)
        keep[:size, :] = mine[here, :] + got[here, :]
        send[:size, :] = mine[there, :] + got[there, :]
        value = mine[2 * size :, :] + got[2 * size :, :]
        keep[size:, :] = value
        send[size:, :] = value


def gram_leaf_kernel(bits, mine0, got0, mine1, got1, keep, send):
    kind = bits[6]
    side = bits[5] == 1
    for s, (mine, got) in enumerate(((mine0, got0), (mine1, got1))):
        n = GRAM[s]
        at = 2 * sum(GRAM[:s])
        put(side, keep, send, at, mine[:n, :] + got[:n, :], mine[n : 2 * n, :] + got[n : 2 * n, :])
        chosen = pl.ds(pl.multiple_of((2 + kind) * n, 8), n)
        put(side, keep, send, at + n, mine[chosen, :] + got[chosen, :], mine[4 * n :, :] + got[4 * n :, :])


def tile_leaf_kernel(bits, mine0, got0, mine1, got1, keep, send):
    side = bits[5] == 1
    for s, (mine, got) in enumerate(((mine0, got0), (mine1, got1))):
        n = TILE[s]
        put(side, keep, send, n * s, mine[:n, :] + got[:n, :], mine[n:, :] + got[n:, :])


def mm(a, b):
    return jnp.dot(a, b, precision=lax.Precision.HIGHEST, preferred_element_type=F32)


def unfold(fold, b, diag):
    r, c = iotas()
    turned = fold.T
    a = jnp.where(r <= c, fold, turned)
    d = jnp.where(r > c, fold, jnp.where(r < c, turned, jnp.broadcast_to(diag, fold.shape)))
    top = jnp.concatenate([a, b], axis=1)
    return jnp.concatenate([top, jnp.concatenate([b.T, d], axis=1)], axis=0)


def residual(gram, count):
    r, c = iotas(MID)
    matrix = gram / count
    level = jnp.sum(jnp.where(r == c, matrix, 0.0)) / MID
    matrix = matrix + jnp.where(r == c, DAMPING * level, 0.0)
    bound = jnp.max(jnp.sum(jnp.abs(matrix), axis=0, keepdims=True))
    return jnp.where(r == c, 1.0, 0.0) - matrix / bound, bound


def inverse_kernel(count, bits, mine, mate, left_out, right_out):
    side = bits[0] == 1
    low = jnp.where(side, mate[...], mine[...])
    high = jnp.where(side, mine[...], mate[...])

    def gram(i):
        starts = [2 * sum(GRAM[:s]) + i * GRAM[s] for s in range(SETS)]
        fold, b = (jnp.concatenate([part[at : at + 64] for at in starts], axis=0) for part in (low, high))
        return unfold(fold, b, low[starts[0] + 64 : starts[0] + 65])

    r, c = iotas(MID)
    own, shared = residual(gram(0), count), residual(gram(1), count)
    powers = [own[0], shared[0]]
    sums = [jnp.where(r == c, 1.0, 0.0) + e for e in powers]
    for step in range(1, NS_ITERS):
        powers = [mm(e, e) for e in powers]
        sums = [x + mm(x, e) for x, e in zip(sums, powers)]
    own, shared = sums[0] / own[1], sums[1] / shared[1]
    third = bits[7] == 1
    left_out[...] = jnp.where(third, shared, own)
    right_out[...] = jnp.where(third, own, shared)


def apply_kernel(count, bits, left, right, mine, mate, out):
    side = bits[0] == 1
    low = jnp.where(side, mate[...], mine[...])
    high = jnp.where(side, mine[...], mate[...])
    tile = jnp.concatenate([low, high], axis=1) / count
    rows = left[pl.ds(pl.multiple_of(bits[0] * HALF, HALF), HALF), :]
    out[...] = mm(mm(rows, tile), right[...]).astype(BF16)


def place_kernel(bits, mine, mate, last, last_mate, out1, out2, out3):
    side = bits[0] == 1
    for half in range(2):
        swap = side if half == 0 else jnp.logical_not(side)
        at = half * HALF
        for j in range(16):
            value = jnp.where(swap, mate[j], mine[j])
            q = tile_of(j // 4, j % 2 * 2 + j // 2 % 2)
            if q < 4:
                out1[q * MID + at : q * MID + at + HALF, :] = value
            elif q < 8:
                out3[at : at + HALF, (q - 4) * MID : (q - 3) * MID] = value
            else:
                out2[(q - 8) * MID + at : (q - 8) * MID + at + HALF, :] = value
        out2[8 * MID + at : 8 * MID + at + HALF, :] = jnp.where(swap, last_mate[...], last[...])


VMEM = pl.BlockSpec(memory_space=pltpu.VMEM)
SMEM = pl.BlockSpec(memory_space=pltpu.SMEM)


def scratch_arrays(scratch):
    return [jax.ShapeDtypeStruct(a.shape, a.dtype) for a in scratch]


def call(kernel, bits, args, outs, scratch=(), flops=0, room=4):
    size = sum(a.size * a.dtype.itemsize for a in args) + sum(o.size * o.dtype.itemsize for o in outs)
    held = sum(a.size * a.dtype.itemsize for a in scratch_arrays(scratch))
    many = len(outs) > 1
    return pl.pallas_call(
        kernel,
        out_shape=tuple(outs) if many else outs[0],
        in_specs=[SMEM] + [VMEM] * len(args),
        out_specs=tuple([VMEM] * len(outs)) if many else VMEM,
        scratch_shapes=list(scratch),
        compiler_params=pltpu.CompilerParams(vmem_limit_bytes=size * 5 // 4 + held + room * 2**20),
        cost_estimate=pl.CostEstimate(flops=flops, bytes_accessed=size, transcendentals=0),
    )(bits, *args)


AXES = ("y", "x_lo", "z", "x_hi", "core")
SIZES = (4, 2, 8, 2, 2)


def place_of(device):
    rep, own = divmod(device, 32)
    return rep // 2, (own // 2) % 2 * 2 + rep % 2, own // 4, own % 2


def device_of(y, x, z, c):
    return (y * 2 + x % 2) * 32 + z * 4 + x // 2 * 2 + c


def route(move):
    return [(d, device_of(*move(*place_of(d)))) for d in range(256)]


ROUTE_C = route(lambda y, x, z, c: (y, x, z, 1 - c))
MOVE = {
    3: lambda y, x, z, c: (y, x ^ 1, z, c),
    2: lambda y, x, z, c: (y, 3 - x, z, c),
    1: lambda y, x, z, c: (y ^ 1, x, z, c),
    0: lambda y, x, z, c: (3 - y, x, z, c),
}
ROUTE_XY = [
    [route(lambda y, x, z, c: MOVE[ORDER[c][s][step]](y, x, z, c)) for step in range(4)] for s in range(SETS)
]
ROUTE_Z1 = route(lambda y, x, z, c: (y, x, z ^ 1, c))
ROUTE_Z2 = route(lambda y, x, z, c: (y, x, 7 - z if c else z ^ 3, c))
ROUTE_Z3 = route(lambda y, x, z, c: (y, x, z ^ 3 if c else 7 - z, c))


def tile_of(y, x):
    return ((x ^ (x >> 1)) & 1) * 8 + (x >> 1) * 4 + ((y ^ (y >> 1)) & 1) * 2 + (y >> 1)


def send_to(value, way):
    return lax.ppermute(value, AXES, way)


def on_device(act_wide, act_middle, act_narrow, grad_first, grad_second, grad_third):
    images, height, width, wide = act_wide.shape
    middle = act_middle.shape[3]
    count = float(images * height * width * 256)
    y, z, core = lax.axis_index("y"), lax.axis_index("z"), lax.axis_index("core")
    x = lax.axis_index("x_hi") * 2 + lax.axis_index("x_lo")
    q = tile_of(y, x)
    own = [(q >> i) & 1 for i in range(4)]
    turns = [jnp.where(core == 1, own[ORDER[1][s][k]], own[ORDER[0][s][k]]) for s in range(SETS) for k in range(4)]
    odd = ((z + 1) >> 1) & 1
    kind = jnp.where(q < 4, 0, jnp.where(q < 8, 1, 2))
    third = jnp.where((kind == 1) & (odd == 0), 1, 0)
    bits = jnp.stack([core, *own, odd, kind, third, q, *turns]).astype(jnp.int32)

    def shape(*dims):
        return jax.ShapeDtypeStruct(dims, F32)

    lines, span = images * height, images * (height + 1)
    pads = [pltpu.VMEM((lines, 16, n), BF16) for n in (wide, middle, middle, wide)]
    maps = [pltpu.VMEM((3, span + 2, 16, middle), BF16), pltpu.VMEM((span, 16, middle), BF16)]
    ends = (act_wide, act_narrow, grad_first, grad_third)
    patches = (act_middle, grad_second)

    def pairs(rec, records):
        return [shape(records * rec[s], HALF) for s in range(SETS) for _ in range(2)]

    def start(rec, many, extra, kernels, bits):
        parts = []
        for part, args, scratch in ((1, patches, maps), (0, ends, pads)):
            outs = [shape(many[part] * sum(rec), HALF)] * 2
            keep, send = call(kernels[part], bits, args, outs, scratch, 2 * many[part] * 900 * 65536)
            parts = [keep, send_to(send, ROUTE_C)] + parts
        outs = pairs(rec, 8 + len(extra))
        return call(functools.partial(first_split_kernel, rec, many, extra), bits, parts, outs)

    def chain(rec, extra, held, leaf):
        for step in range(4):
            args = []
            for s in range(SETS):
                args += [held[2 * s], send_to(held[2 * s + 1], ROUTE_XY[s][step])]
            if step < 3:
                held = call(functools.partial(split_kernel, rec, step + 1), bits, args, pairs(rec, (4 >> step) + extra))
        size = sum(rec) * (1 if extra == 1 else 2)
        keep, send = call(leaf, bits, args, [shape(size, HALF)] * 2)
        total = keep + send_to(send, ROUTE_Z1)
        total = total + send_to(total, ROUTE_Z2)
        total = total + send_to(total, ROUTE_Z3)
        return total, send_to(total, ROUTE_C)

    shared = ((1, 8), (0, 8), (0, 9), (1, 9))
    held = start(GRAM, (10, 10), shared, (end_grams_kernel, patch_grams_kernel), bits)
    *held, later = lax.optimization_barrier((*held, bits))
    grams = chain(GRAM, 4, held, gram_leaf_kernel)
    held = start(TILE, (8, 9), ((1, 8),), (end_tiles_kernel, patch_tiles_kernel), later)
    tiles = chain(TILE, 1, held, tile_leaf_kernel)
    inverses = call(
        functools.partial(inverse_kernel, count),
        bits,
        grams,
        [shape(MID, MID)] * 2,
        flops=2 * 20 * 6 * MID**3,
        room=16,
    )
    mine = call(
        functools.partial(apply_kernel, count),
        bits,
        (*inverses, *tiles),
        [jax.ShapeDtypeStruct((HALF, MID), BF16)],
        flops=2 * 6 * MID**3,
    )
    other = send_to(mine, ROUTE_Z1)
    tile, last = jnp.where(odd == 0, mine, other), jnp.where(odd == 0, other, mine)
    tiles = jnp.broadcast_to(tile[None], (16, HALF, MID))
    tiles = lax.all_to_all(tiles, ("y", "x_lo", "x_hi"), 0, 0)
    pieces = (tiles, send_to(tiles, ROUTE_C), last, send_to(last, ROUTE_C))
    outs = [
        jax.ShapeDtypeStruct((wide, middle), BF16),
        jax.ShapeDtypeStruct((9 * middle, middle), BF16),
        jax.ShapeDtypeStruct((middle, wide), BF16),
    ]
    return call(place_kernel, bits, pieces, outs)


def solution(mesh):
    mesh = Mesh(mesh.devices.reshape(SIZES), AXES)
    placed = P(AXES, None, None, None)
    return jax.shard_map(on_device, mesh=mesh, in_specs=(placed,) * 6, out_specs=(P(), P(), P()), check_vma=False)
```

```python
import functools

import jax
import jax.numpy as jnp
from jax import lax
from jax.experimental import pallas as pl
from jax.experimental.pallas import tpu as pltpu
from jax.sharding import Mesh
from jax.sharding import PartitionSpec as P

NS_ITERS = 6
DAMPING = 0.1
MID = 256
HALF = 128
SETS = 2
F32 = jnp.float32
BF16 = jnp.bfloat16

GRAM = (72, 64)
TILE = (128, 128)
ORDER = (((3, 2, 1, 0), (1, 0, 3, 2)), ((2, 3, 0, 1), (0, 1, 2, 3)))
def slot(order, q):
    return sum(((q >> order[k]) & 1) << (3 - k) for k in range(4))


def dot_t(a, b):
    return lax.dot_general(a, b, (((0,), (0,)), ((), ())), preferred_element_type=F32)


def iotas(n=HALF):
    return lax.broadcasted_iota(jnp.int32, (n, n), 0), lax.broadcasted_iota(jnp.int32, (n, n), 1)


def put(side, keep, send, at, low, high):
    n = low.shape[0]
    keep[at : at + n, :] = jnp.where(side, high, low)
    send[at : at + n, :] = jnp.where(side, low, high)


def put_gram(side, keep, send, many, i, gram):
    r, c = iotas()
    a, b, d = gram[:HALF, :HALF], gram[:HALF, HALF:], gram[HALF:, HALF:]
    fold = jnp.where(r <= c, a, d)
    for s in range(SETS):
        at = many * sum(GRAM[:s]) + i * GRAM[s]
        put(side, keep, send, at, fold[64 * s : 64 * s + 64], b[64 * s : 64 * s + 64])
    diag = jnp.broadcast_to(jnp.sum(jnp.where(r == c, d, 0.0), axis=0, keepdims=True), (8, HALF))
    put(side, keep, send, i * GRAM[0] + 64, diag, diag)


def put_tile(side, keep, send, many, i, tile):
    for s in range(SETS):
        rows = tile[HALF * s : HALF * s + HALF]
        put(side, keep, send, many * sum(TILE[:s]) + i * TILE[s], rows[:, :HALF], rows[:, HALF:])


def columns(ref, k=0):
    h, w, n, _ = ref.shape
    return ref[:, :, :, MID * k : MID * k + MID].reshape(h * w * n, MID)


def end_grams_kernel(bits, aw, an, g1, g3, keep, send):
    side = bits[0] == 1
    blocks = [(aw, k) for k in range(4)] + [(g3, k) for k in range(4)] + [(g1, 0), (an, 0)]
    for i, block in enumerate(blocks):
        own = columns(*block)
        put_gram(side, keep, send, 10, i, dot_t(own, own))


def end_tiles_kernel(bits, aw, an, g1, g3, keep, send):
    side = bits[0] == 1
    first_out, third_in = columns(g1), columns(an)
    for q in range(8):
        tile = dot_t(columns(aw, q), first_out) if q < 4 else dot_t(third_in, columns(g3, q - 4))
        put_tile(side, keep, send, 8, q, tile)


def widen(value, before):
    h, w, n, c = value.shape
    blank = lambda k: [jnp.zeros((h, k, n, c), BF16)] if k else []
    return jnp.concatenate(blank(before) + [value] + blank(16 - w - before), axis=1).reshape(h * 16 * n, c)


def shift(am, lines):
    h, w, n, c = am.shape
    step = 16 * n
    whole = am[...]
    for dx, moved in enumerate((widen(whole[:, : w - 1], 1), widen(whole, 0), widen(whole[:, 1:], 0))):
        lines[dx, :step, :] = jnp.zeros((step, c), BF16)
        lines[dx, step : step + h * step, :] = moved
        lines[dx, step + h * step :, :] = jnp.zeros((step, c), BF16)
    return step


def patch_grams_kernel(bits, am, g2, keep, send, lines):
    side = bits[0] == 1
    step = shift(am, lines)
    second_out = columns(g2)
    put_gram(side, keep, send, 10, 9, dot_t(second_out, second_out))
    end = step * (am.shape[0] + 1)
    for dx in range(3):
        cuts = (step, 2 * step), (2 * step, end - step), (end - step, end)
        top, inner, bottom = (dot_t(lines[dx, lo:hi, :], lines[dx, lo:hi, :]) for lo, hi in cuts)
        upper = inner + top
        put_gram(side, keep, send, 10, dx, upper)
        put_gram(side, keep, send, 10, 3 + dx, upper + bottom)
        put_gram(side, keep, send, 10, 6 + dx, inner + bottom)


def patch_tiles_kernel(bits, am, g2, keep, send, lines):
    side = bits[0] == 1
    step = shift(am, lines)
    second_out = widen(g2[...], 0)
    span = second_out.shape[0]
    for q in range(9):
        at = step * (q // 3)
        put_tile(side, keep, send, 9, q, dot_t(lines[q % 3, at : at + span, :], second_out))


def first_split_kernel(rec, many, extra, bits, keep0, got0, keep1, got1, *outs):
    for core in range(2):

        @pl.when(bits[0] == core)
        def _(core=core):
            first_split(ORDER[core], rec, many, extra, bits, ((keep0, got0), (keep1, got1)), outs)


def first_split(orders, rec, many, extra, bits, parts, outs):
    for s in range(SETS):
        keep, send = outs[2 * s], outs[2 * s + 1]
        lead = orders[s][0]
        side = bits[1 + lead] == 1
        n = rec[s]

        def summed(part, i):
            mine, got = parts[part]
            at = many[part] * sum(rec[:s]) + i * n
            return mine[at : at + n, :] + got[at : at + n, :]

        for q in range(16):
            if (q >> lead) & 1:
                continue
            other = q | 1 << lead
            put(side, keep, send, slot(orders[s], q) * n, summed(q // 8, q % 8), summed(other // 8, other % 8))
        for i, (part, j) in enumerate(extra):
            value = summed(part, j)
            keep[(8 + i) * n : (9 + i) * n, :] = value
            send[(8 + i) * n : (9 + i) * n, :] = value


def split_kernel(rec, step, bits, *refs):
    tiles = 16 >> step
    for s in range(SETS):
        mine, got = refs[2 * s], refs[2 * s + 1]
        keep, send = refs[2 * SETS + 2 * s], refs[2 * SETS + 2 * s + 1]
        size = (tiles // 2) * rec[s]
        bit = bits[9 + 4 * s + step]
        here = pl.ds(pl.multiple_of(bit * size, 8), size)
        there = pl.ds(pl.multiple_of((1 - bit) * size, 8), size)
        keep[:size, :] = mine[here, :] + got[here, :]
        send[:size, :] = mine[there, :] + got[there, :]
        value = mine[2 * size :, :] + got[2 * size :, :]
        keep[size:, :] = value
        send[size:, :] = value


def gram_leaf_kernel(bits, mine0, got0, mine1, got1, keep, send):
    kind = bits[6]
    side = bits[5] == 1
    for s, (mine, got) in enumerate(((mine0, got0), (mine1, got1))):
        n = GRAM[s]
        at = 2 * sum(GRAM[:s])
        put(side, keep, send, at, mine[:n, :] + got[:n, :], mine[n : 2 * n, :] + got[n : 2 * n, :])
        chosen = pl.ds(pl.multiple_of((2 + kind) * n, 8), n)
        put(side, keep, send, at + n, mine[chosen, :] + got[chosen, :], mine[4 * n :, :] + got[4 * n :, :])


def tile_leaf_kernel(bits, mine0, got0, mine1, got1, keep, send):
    side = bits[5] == 1
    for s, (mine, got) in enumerate(((mine0, got0), (mine1, got1))):
        n = TILE[s]
        put(side, keep, send, n * s, mine[:n, :] + got[:n, :], mine[n:, :] + got[n:, :])


def halves(x):
    high = x.astype(BF16)
    return high, (x - high.astype(F32)).astype(BF16)


def mm3(a, b):
    (ah, al), (bh, bl) = halves(a), halves(b)
    return jnp.dot(ah, bh, preferred_element_type=F32) + (
        jnp.dot(ah, bl, preferred_element_type=F32) + jnp.dot(al, bh, preferred_element_type=F32)
    )


def mm(a, b):
    return jnp.dot(a, b, precision=lax.Precision.HIGHEST, preferred_element_type=F32)


def unfold(fold, b, diag):
    r, c = iotas()
    turned = fold.T
    a = jnp.where(r <= c, fold, turned)
    d = jnp.where(r > c, fold, jnp.where(r < c, turned, jnp.broadcast_to(diag, fold.shape)))
    top = jnp.concatenate([a, b], axis=1)
    return jnp.concatenate([top, jnp.concatenate([b.T, d], axis=1)], axis=0)


def residual(gram, count):
    r, c = iotas(MID)
    matrix = gram / count
    level = jnp.sum(jnp.where(r == c, matrix, 0.0)) / MID
    matrix = matrix + jnp.where(r == c, DAMPING * level, 0.0)
    bound = jnp.max(jnp.sum(jnp.abs(matrix), axis=0, keepdims=True))
    return jnp.where(r == c, 1.0, 0.0) - matrix / bound, bound


def inverse_kernel(count, bits, mine, mate, left_out, right_out):
    side = bits[0] == 1
    low = jnp.where(side, mate[...], mine[...])
    high = jnp.where(side, mine[...], mate[...])

    def gram(i):
        starts = [2 * sum(GRAM[:s]) + i * GRAM[s] for s in range(SETS)]
        fold, b = (jnp.concatenate([part[at : at + 64] for at in starts], axis=0) for part in (low, high))
        return unfold(fold, b, low[starts[0] + 64 : starts[0] + 65])

    r, c = iotas(MID)
    own, shared = residual(gram(0), count), residual(gram(1), count)
    powers = [own[0], shared[0]]
    sums = [jnp.where(r == c, 1.0, 0.0) + e for e in powers]
    for step in range(1, NS_ITERS):
        times = mm if step < 3 else mm3
        powers = [times(e, e) for e in powers]
        sums = [x + mm3(x, e) for x, e in zip(sums, powers)]
    own, shared = sums[0] / own[1], sums[1] / shared[1]
    third = bits[7] == 1
    left_out[...] = jnp.where(third, shared, own)
    right_out[...] = jnp.where(third, own, shared)


def apply_kernel(count, bits, left, right, mine, mate, out):
    side = bits[0] == 1
    low = jnp.where(side, mate[...], mine[...])
    high = jnp.where(side, mine[...], mate[...])
    tile = jnp.concatenate([low, high], axis=1) / count
    rows = left[pl.ds(pl.multiple_of(bits[0] * HALF, HALF), HALF), :]
    out[...] = mm(mm(rows, tile), right[...]).astype(BF16)


def place_kernel(bits, mine, mate, last, last_mate, out1, out2, out3):
    side = bits[0] == 1
    for half in range(2):
        swap = side if half == 0 else jnp.logical_not(side)
        at = half * HALF
        for j in range(16):
            value = jnp.where(swap, mate[j], mine[j])
            q = tile_of(j // 4, j % 2 * 2 + j // 2 % 2)
            if q < 4:
                out1[q * MID + at : q * MID + at + HALF, :] = value
            elif q < 8:
                out3[at : at + HALF, (q - 4) * MID : (q - 3) * MID] = value
            else:
                out2[(q - 8) * MID + at : (q - 8) * MID + at + HALF, :] = value
        out2[8 * MID + at : 8 * MID + at + HALF, :] = jnp.where(swap, last_mate[...], last[...])


VMEM = pl.BlockSpec(memory_space=pltpu.VMEM)
SMEM = pl.BlockSpec(memory_space=pltpu.SMEM)


def scratch_arrays(scratch):
    return [jax.ShapeDtypeStruct(a.shape, a.dtype) for a in scratch]


def call(kernel, bits, args, outs, scratch=(), flops=0, room=4):
    size = sum(a.size * a.dtype.itemsize for a in args) + sum(o.size * o.dtype.itemsize for o in outs)
    held = sum(a.size * a.dtype.itemsize for a in scratch_arrays(scratch))
    many = len(outs) > 1
    return pl.pallas_call(
        kernel,
        out_shape=tuple(outs) if many else outs[0],
        in_specs=[SMEM] + [VMEM] * len(args),
        out_specs=tuple([VMEM] * len(outs)) if many else VMEM,
        scratch_shapes=list(scratch),
        compiler_params=pltpu.CompilerParams(vmem_limit_bytes=size * 5 // 4 + held + room * 2**20),
        cost_estimate=pl.CostEstimate(flops=flops, bytes_accessed=size if flops else 1024, transcendentals=0),
    )(bits, *args)


AXES = ("y", "x_lo", "z", "x_hi", "core")
SIZES = (4, 2, 8, 2, 2)


def place_of(device):
    rep, own = divmod(device, 32)
    return rep // 2, (own // 2) % 2 * 2 + rep % 2, own // 4, own % 2


def device_of(y, x, z, c):
    return (y * 2 + x % 2) * 32 + z * 4 + x // 2 * 2 + c


def route(move):
    return [(d, device_of(*move(*place_of(d)))) for d in range(256)]


ROUTE_C = route(lambda y, x, z, c: (y, x, z, 1 - c))
MOVE = {
    3: lambda y, x, z, c: (y, x ^ 1, z, c),
    2: lambda y, x, z, c: (y, 3 - x, z, c),
    1: lambda y, x, z, c: (y ^ 1, x, z, c),
    0: lambda y, x, z, c: (3 - y, x, z, c),
}
ROUTE_XY = [
    [route(lambda y, x, z, c: MOVE[ORDER[c][s][step]](y, x, z, c)) for step in range(4)] for s in range(SETS)
]
STEP_Z = (
    lambda z: z ^ 1,
    lambda z: z - 1 + 2 * (z % 2),
    lambda z: z ^ 2,
    lambda z: z - 2 + 4 * (z // 2 % 2),
)
ROUTE_Z1, ROUTE_Z2, ROUTE_Z3 = (
    [(d, device_of(*(lambda y, x, z, c: (y, x, STEP_Z[pair[c]](z) % 8, c))(*place_of(d)))) for d in range(256)]
    for pair in ((0, 1), (2, 3), (3, 2))
)


def tile_of(y, x):
    return ((x ^ (x >> 1)) & 1) * 8 + (x >> 1) * 4 + ((y ^ (y >> 1)) & 1) * 2 + (y >> 1)


def send_to(value, way):
    return lax.ppermute(value, AXES, way)


def on_device(act_wide, act_middle, act_narrow, grad_first, grad_second, grad_third):
    images, height, width, wide = act_wide.shape
    middle = act_middle.shape[3]
    count = float(images * height * width * 256)
    y, z, core = lax.axis_index("y"), lax.axis_index("z"), lax.axis_index("core")
    x = lax.axis_index("x_hi") * 2 + lax.axis_index("x_lo")
    q = tile_of(y, x)
    own = [(q >> i) & 1 for i in range(4)]
    turns = [jnp.where(core == 1, own[ORDER[1][s][k]], own[ORDER[0][s][k]]) for s in range(SETS) for k in range(4)]
    odd = z & 1
    kind = jnp.where(q < 4, 0, jnp.where(q < 8, 1, 2))
    third = jnp.where((kind == 1) & (odd == 0), 1, 0)
    bits = jnp.stack([core, *own, odd, kind, third, q, *turns]).astype(jnp.int32)

    def shape(*dims):
        return jax.ShapeDtypeStruct(dims, F32)

    maps = [pltpu.VMEM((3, (height + 2) * 16 * images, middle), BF16)]
    ends = [a.transpose(1, 2, 0, 3) for a in (act_wide, act_narrow, grad_first, grad_third)]
    patches = [a.transpose(1, 2, 0, 3) for a in (act_middle, grad_second)]

    def pairs(rec, records):
        return [shape(records * rec[s], HALF) for s in range(SETS) for _ in range(2)]

    def start(rec, many, extra, kernels, bits):
        parts = []
        for part, args, scratch in ((1, patches, maps), (0, ends, ())):
            outs = [shape(many[part] * sum(rec), HALF)] * 2
            keep, send = call(kernels[part], bits[part], args, outs, scratch, 2 * many[part] * 900 * 65536)
            parts = [keep, send_to(send, ROUTE_C)] + parts
        return parts

    def begin(rec, many, extra, parts):
        outs = pairs(rec, 8 + len(extra))
        return call(functools.partial(first_split_kernel, rec, many, extra), bits, parts, outs)

    def chain(rec, extra, held, leaf, meanwhile=()):
        for step in range(4):
            args = []
            for s in range(SETS):
                args += [held[2 * s], send_to(held[2 * s + 1], ROUTE_XY[s][step])]
            if step < 3:
                held = call(functools.partial(split_kernel, rec, step + 1), bits, args, pairs(rec, (4 >> step) + extra))
        size = sum(rec) * (1 if extra == 1 else 2)
        keep, send = call(leaf, bits, args, [shape(size, HALF)] * 2)
        total = keep + send_to(send, ROUTE_Z1)
        total = total + send_to(total, ROUTE_Z2)
        got, *meanwhile = lax.optimization_barrier((send_to(total, ROUTE_Z3), *meanwhile))
        total = total + got
        return (total, send_to(total, ROUTE_C), *meanwhile)

    shared = ((1, 8), (0, 8), (0, 9), (1, 9))
    gram_parts = start(GRAM, (10, 10), shared, (end_grams_kernel, patch_grams_kernel), (bits, bits))
    got0, later0 = lax.optimization_barrier((gram_parts[1], bits))
    got1, later1 = lax.optimization_barrier((gram_parts[3], bits))
    gram_parts = [gram_parts[0], got0, gram_parts[2], got1]
    tile_parts = start(TILE, (8, 9), ((1, 8),), (end_tiles_kernel, patch_tiles_kernel), (later0, later1))
    held = begin(GRAM, (10, 10), shared, gram_parts)
    grams = chain(GRAM, 4, held, gram_leaf_kernel)
    held = begin(TILE, (8, 9), ((1, 8),), tile_parts)
    inverses = call(
        functools.partial(inverse_kernel, count),
        bits,
        grams,
        [shape(MID, MID)] * 2,
        room=16,
    )
    *tiles, left, right = chain(TILE, 1, held, tile_leaf_kernel, inverses)
    mine = call(
        functools.partial(apply_kernel, count),
        bits,
        (left, right, *tiles),
        [jax.ShapeDtypeStruct((HALF, MID), BF16)],
    )
    other = send_to(mine, ROUTE_Z1)
    tile, last = jnp.where(odd == 0, mine, other), jnp.where(odd == 0, other, mine)
    tiles = jnp.broadcast_to(tile[None], (16, HALF, MID))
    tiles = lax.all_to_all(tiles, ("y", "x_lo", "x_hi"), 0, 0)
    pieces = (tiles, send_to(tiles, ROUTE_C), last, send_to(last, ROUTE_C))
    outs = [
        jax.ShapeDtypeStruct((wide, middle), BF16),
        jax.ShapeDtypeStruct((9 * middle, middle), BF16),
        jax.ShapeDtypeStruct((middle, wide), BF16),
    ]
    return call(place_kernel, bits, pieces, outs)


def solution(mesh):
    mesh = Mesh(mesh.devices.reshape(SIZES), AXES)
    placed = P(AXES, None, None, None)
    return jax.shard_map(on_device, mesh=mesh, in_specs=(placed,) * 6, out_specs=(P(), P(), P()), check_vma=False)
```

```python
import functools

import jax
import jax.numpy as jnp
from jax import lax
from jax.experimental import pallas as pl
from jax.experimental.pallas import tpu as pltpu
from jax.sharding import Mesh
from jax.sharding import PartitionSpec as P

NS_ITERS = 6
DAMPING = 0.1
MID = 256
HALF = 128
SETS = 2
F32 = jnp.float32
BF16 = jnp.bfloat16

GRAM = (72, 64)
TILE = (128, 128)
ORDER = (((3, 2, 1, 0), (1, 0, 3, 2)), ((2, 3, 0, 1), (0, 1, 2, 3)))
def slot(order, q):
    return sum(((q >> order[k]) & 1) << (3 - k) for k in range(4))


def dot_t(a, b):
    return lax.dot_general(a, b, (((0,), (0,)), ((), ())), preferred_element_type=F32)


def iotas(n=HALF):
    return lax.broadcasted_iota(jnp.int32, (n, n), 0), lax.broadcasted_iota(jnp.int32, (n, n), 1)


def put(side, keep, send, at, low, high):
    n = low.shape[0]
    keep[at : at + n, :] = jnp.where(side, high, low)
    send[at : at + n, :] = jnp.where(side, low, high)


def put_gram(side, keep, send, many, i, gram):
    r, c = iotas()
    a, b, d = gram[:HALF, :HALF], gram[:HALF, HALF:], gram[HALF:, HALF:]
    fold = jnp.where(r <= c, a, d)
    for s in range(SETS):
        at = many * sum(GRAM[:s]) + i * GRAM[s]
        put(side, keep, send, at, fold[64 * s : 64 * s + 64], b[64 * s : 64 * s + 64])
    diag = jnp.broadcast_to(jnp.sum(jnp.where(r == c, d, 0.0), axis=0, keepdims=True), (8, HALF))
    put(side, keep, send, i * GRAM[0] + 64, diag, diag)


def put_tile(side, keep, send, many, i, tile):
    for s in range(SETS):
        rows = tile[HALF * s : HALF * s + HALF]
        put(side, keep, send, many * sum(TILE[:s]) + i * TILE[s], rows[:, :HALF], rows[:, HALF:])


def columns(ref, k=0):
    h, w, n, _ = ref.shape
    return ref[:, :, :, MID * k : MID * k + MID].reshape(h * w * n, MID)


def end_grams_kernel(bits, aw, an, g1, g3, keep, send):
    side = bits[0] == 1
    blocks = [(aw, k) for k in range(4)] + [(g3, k) for k in range(4)] + [(g1, 0), (an, 0)]
    for i, block in enumerate(blocks):
        own = columns(*block)
        put_gram(side, keep, send, 10, i, dot_t(own, own))


def end_tiles_kernel(bits, aw, an, g1, g3, keep, send):
    side = bits[0] == 1
    first_out, third_in = columns(g1), columns(an)
    for q in range(8):
        tile = dot_t(columns(aw, q), first_out) if q < 4 else dot_t(third_in, columns(g3, q - 4))
        put_tile(side, keep, send, 8, q, tile)


def widen(value, before):
    h, w, n, c = value.shape
    blank = lambda k: [jnp.zeros((h, k, n, c), BF16)] if k else []
    return jnp.concatenate(blank(before) + [value] + blank(16 - w - before), axis=1).reshape(h * 16 * n, c)


def shift(am, lines):
    h, w, n, c = am.shape
    step = 16 * n
    for dx, moved in enumerate((widen(am[:, : w - 1], 1), widen(am, 0), widen(am[:, 1:], 0))):
        lines[dx, :step, :] = jnp.zeros((step, c), BF16)
        lines[dx, step : step + h * step, :] = moved
        lines[dx, step + h * step :, :] = jnp.zeros((step, c), BF16)
    return step


def patch_grams_kernel(bits, both, keep, send, lines):
    side = bits[0] == 1
    am, g2 = both[: both.shape[0] // 2], both[both.shape[0] // 2 :]
    step = shift(am, lines)
    second_out = columns(g2)
    put_gram(side, keep, send, 10, 9, dot_t(second_out, second_out))
    end = step * (am.shape[0] + 1)
    for dx in range(3):
        cuts = (step, 2 * step), (2 * step, end - step), (end - step, end)
        top, inner, bottom = (dot_t(lines[dx, lo:hi, :], lines[dx, lo:hi, :]) for lo, hi in cuts)
        upper = inner + top
        put_gram(side, keep, send, 10, dx, upper)
        put_gram(side, keep, send, 10, 3 + dx, upper + bottom)
        put_gram(side, keep, send, 10, 6 + dx, inner + bottom)


def patch_tiles_kernel(bits, both, keep, send, lines):
    side = bits[0] == 1
    am, g2 = both[: both.shape[0] // 2], both[both.shape[0] // 2 :]
    step = shift(am, lines)
    second_out = widen(g2, 0)
    span = second_out.shape[0]
    for q in range(9):
        at = step * (q // 3)
        put_tile(side, keep, send, 9, q, dot_t(lines[q % 3, at : at + span, :], second_out))


def first_split_kernel(rec, many, extra, bits, keep0, got0, keep1, got1, *outs):
    for core in range(2):

        @pl.when(bits[0] == core)
        def _(core=core):
            first_split(ORDER[core], rec, many, extra, bits, ((keep0, got0), (keep1, got1)), outs)


def first_split(orders, rec, many, extra, bits, parts, outs):
    for s in range(SETS):
        keep, send = outs[2 * s], outs[2 * s + 1]
        lead = orders[s][0]
        side = bits[1 + lead] == 1
        n = rec[s]

        def summed(part, i):
            mine, got = parts[part]
            at = many[part] * sum(rec[:s]) + i * n
            return mine[at : at + n, :] + got[at : at + n, :]

        for q in range(16):
            if (q >> lead) & 1:
                continue
            other = q | 1 << lead
            put(side, keep, send, slot(orders[s], q) * n, summed(q // 8, q % 8), summed(other // 8, other % 8))
        for i, (part, j) in enumerate(extra):
            value = summed(part, j)
            keep[(8 + i) * n : (9 + i) * n, :] = value
            send[(8 + i) * n : (9 + i) * n, :] = value


def split_kernel(rec, step, bits, *refs):
    tiles = 16 >> step
    for s in range(SETS):
        mine, got = refs[2 * s], refs[2 * s + 1]
        keep, send = refs[2 * SETS + 2 * s], refs[2 * SETS + 2 * s + 1]
        size = (tiles // 2) * rec[s]
        bit = bits[9 + 4 * s + step]
        here = pl.ds(pl.multiple_of(bit * size, 8), size)
        there = pl.ds(pl.multiple_of((1 - bit) * size, 8), size)
        keep[:size, :] = mine[here, :] + got[here, :]
        send[:size, :] = mine[there, :] + got[there, :]
        value = mine[2 * size :, :] + got[2 * size :, :]
        keep[size:, :] = value
        send[size:, :] = value


def gram_leaf_kernel(bits, mine0, got0, mine1, got1, keep, send):
    kind = bits[6]
    side = bits[5] == 1
    for s, (mine, got) in enumerate(((mine0, got0), (mine1, got1))):
        n = GRAM[s]
        at = 2 * sum(GRAM[:s])
        put(side, keep, send, at, mine[:n, :] + got[:n, :], mine[n : 2 * n, :] + got[n : 2 * n, :])
        chosen = pl.ds(pl.multiple_of((2 + kind) * n, 8), n)
        put(side, keep, send, at + n, mine[chosen, :] + got[chosen, :], mine[4 * n :, :] + got[4 * n :, :])


def tile_leaf_kernel(bits, mine0, got0, mine1, got1, keep, send):
    side = bits[5] == 1
    for s, (mine, got) in enumerate(((mine0, got0), (mine1, got1))):
        n = TILE[s]
        put(side, keep, send, n * s, mine[:n, :] + got[:n, :], mine[n:, :] + got[n:, :])


def halves(x):
    high = x.astype(BF16)
    return high, (x - high.astype(F32)).astype(BF16)


def mm3(a, b):
    (ah, al), (bh, bl) = halves(a), halves(b)
    return jnp.dot(ah, bh, preferred_element_type=F32) + (
        jnp.dot(ah, bl, preferred_element_type=F32) + jnp.dot(al, bh, preferred_element_type=F32)
    )


def mm(a, b):
    return jnp.dot(a, b, precision=lax.Precision.HIGHEST, preferred_element_type=F32)


def unfold(fold, b, diag):
    r, c = iotas()
    turned = fold.T
    a = jnp.where(r <= c, fold, turned)
    d = jnp.where(r > c, fold, jnp.where(r < c, turned, jnp.broadcast_to(diag, fold.shape)))
    top = jnp.concatenate([a, b], axis=1)
    return jnp.concatenate([top, jnp.concatenate([b.T, d], axis=1)], axis=0)


def residual(gram, count):
    r, c = iotas(MID)
    matrix = gram / count
    level = jnp.sum(jnp.where(r == c, matrix, 0.0)) / MID
    matrix = matrix + jnp.where(r == c, DAMPING * level, 0.0)
    bound = jnp.max(jnp.sum(jnp.abs(matrix), axis=0, keepdims=True))
    return jnp.where(r == c, 1.0, 0.0) - matrix / bound, bound


def inverse_kernel(count, bits, mine, mate, left_out, right_out):
    side = bits[0] == 1
    low = jnp.where(side, mate[...], mine[...])
    high = jnp.where(side, mine[...], mate[...])

    def gram(i):
        starts = [2 * sum(GRAM[:s]) + i * GRAM[s] for s in range(SETS)]
        fold, b = (jnp.concatenate([part[at : at + 64] for at in starts], axis=0) for part in (low, high))
        return unfold(fold, b, low[starts[0] + 64 : starts[0] + 65])

    r, c = iotas(MID)
    own, shared = residual(gram(0), count), residual(gram(1), count)
    powers = [own[0], shared[0]]
    sums = [jnp.where(r == c, 1.0, 0.0) + e for e in powers]
    for step in range(1, NS_ITERS):
        times = mm if step < 3 else mm3
        powers = [times(e, e) for e in powers]
        sums = [x + mm3(x, e) for x, e in zip(sums, powers)]
    own, shared = sums[0] / own[1], sums[1] / shared[1]
    third = bits[7] == 1
    left_out[...] = jnp.where(third, shared, own)
    right_out[...] = jnp.where(third, own, shared)


def apply_kernel(count, bits, left, right, mine, mate, out):
    side = bits[0] == 1
    low = jnp.where(side, mate[...], mine[...])
    high = jnp.where(side, mine[...], mate[...])
    tile = jnp.concatenate([low, high], axis=1) / count
    rows = left[pl.ds(pl.multiple_of(bits[0] * HALF, HALF), HALF), :]
    out[...] = mm(mm(rows, tile), right[...]).astype(BF16)


def place_kernel(bits, mine, mate, last, last_mate, out1, out2, out3):
    side = bits[0] == 1
    for half in range(2):
        swap = side if half == 0 else jnp.logical_not(side)
        at = half * HALF
        for j in range(16):
            value = jnp.where(swap, mate[j], mine[j])
            q = tile_of(j // 4, j % 2 * 2 + j // 2 % 2)
            if q < 4:
                out1[q * MID + at : q * MID + at + HALF, :] = value
            elif q < 8:
                out3[at : at + HALF, (q - 4) * MID : (q - 3) * MID] = value
            else:
                out2[(q - 8) * MID + at : (q - 8) * MID + at + HALF, :] = value
        out2[8 * MID + at : 8 * MID + at + HALF, :] = jnp.where(swap, last_mate[...], last[...])


VMEM = pl.BlockSpec(memory_space=pltpu.VMEM)
SMEM = pl.BlockSpec(memory_space=pltpu.SMEM)


def scratch_arrays(scratch):
    return [jax.ShapeDtypeStruct(a.shape, a.dtype) for a in scratch]


def call(kernel, bits, args, outs, scratch=(), flops=0, room=4):
    size = sum(a.size * a.dtype.itemsize for a in args) + sum(o.size * o.dtype.itemsize for o in outs)
    held = sum(a.size * a.dtype.itemsize for a in scratch_arrays(scratch))
    many = len(outs) > 1
    return pl.pallas_call(
        kernel,
        out_shape=tuple(outs) if many else outs[0],
        in_specs=[SMEM] + [VMEM] * len(args),
        out_specs=tuple([VMEM] * len(outs)) if many else VMEM,
        scratch_shapes=list(scratch),
        compiler_params=pltpu.CompilerParams(vmem_limit_bytes=size * 5 // 4 + held + room * 2**20),
        cost_estimate=pl.CostEstimate(flops=flops or 7 * 10**8, bytes_accessed=size if flops else 1024, transcendentals=0),
    )(bits, *args)


AXES = ("y", "x_lo", "z", "x_hi", "core")
SIZES = (4, 2, 8, 2, 2)


def place_of(device):
    rep, own = divmod(device, 32)
    return rep // 2, (own // 2) % 2 * 2 + rep % 2, own // 4, own % 2


def device_of(y, x, z, c):
    return (y * 2 + x % 2) * 32 + z * 4 + x // 2 * 2 + c


def route(move):
    return [(d, device_of(*move(*place_of(d)))) for d in range(256)]


ROUTE_C = route(lambda y, x, z, c: (y, x, z, 1 - c))
MOVE = {
    3: lambda y, x, z, c: (y, x ^ 1, z, c),
    2: lambda y, x, z, c: (y, 3 - x, z, c),
    1: lambda y, x, z, c: (y ^ 1, x, z, c),
    0: lambda y, x, z, c: (3 - y, x, z, c),
}
ROUTE_XY = [
    [route(lambda y, x, z, c: MOVE[ORDER[c][s][step]](y, x, z, c)) for step in range(4)] for s in range(SETS)
]
ROUTE_Z1 = route(lambda y, x, z, c: (y, x, z ^ 1, c))
ROUTE_Z2 = route(lambda y, x, z, c: (y, x, (z - 1 + 2 * (z % 2)) % 8, c))
ROUTE_Z3 = route(lambda y, x, z, c: (y, x, (3, 6, 5, 0, 7, 2, 1, 4)[z], c))


def tile_of(y, x):
    return ((x ^ (x >> 1)) & 1) * 8 + (x >> 1) * 4 + ((y ^ (y >> 1)) & 1) * 2 + (y >> 1)


def send_to(value, way):
    return lax.ppermute(value, AXES, way)


def on_device(act_wide, act_middle, act_narrow, grad_first, grad_second, grad_third):
    images, height, width, wide = act_wide.shape
    middle = act_middle.shape[3]
    count = float(images * height * width * 256)
    y, z, core = lax.axis_index("y"), lax.axis_index("z"), lax.axis_index("core")
    x = lax.axis_index("x_hi") * 2 + lax.axis_index("x_lo")
    q = tile_of(y, x)
    own = [(q >> i) & 1 for i in range(4)]
    turns = [jnp.where(core == 1, own[ORDER[1][s][k]], own[ORDER[0][s][k]]) for s in range(SETS) for k in range(4)]
    odd = ((z + 1) >> 1) & 1
    kind = jnp.where(q < 4, 0, jnp.where(q < 8, 1, 2))
    third = jnp.where((kind == 1) & (odd == 0), 1, 0)
    bits = jnp.stack([core, *own, odd, kind, third, q, *turns]).astype(jnp.int32)

    def shape(*dims):
        return jax.ShapeDtypeStruct(dims, F32)

    maps = [pltpu.VMEM((3, (height + 2) * 16 * images, middle), BF16)]
    ends = [a.transpose(1, 2, 0, 3) for a in (act_wide, act_narrow, grad_first, grad_third)]
    patches = [jnp.concatenate([a.transpose(1, 2, 0, 3) for a in (act_middle, grad_second)], axis=0)]

    def pairs(rec, records):
        return [shape(records * rec[s], HALF) for s in range(SETS) for _ in range(2)]

    def start(rec, many, extra, kernels, bits):
        parts = []
        for part, args, scratch in ((1, patches, maps), (0, ends, ())):
            outs = [shape(many[part] * sum(rec), HALF)] * 2
            keep, send = call(kernels[part], bits[part], args, outs, scratch, 2 * many[part] * 900 * 65536)
            parts = [keep, send_to(send, ROUTE_C)] + parts
        return parts

    def begin(rec, many, extra, parts):
        outs = pairs(rec, 8 + len(extra))
        return call(functools.partial(first_split_kernel, rec, many, extra), bits, parts, outs)

    def chain(rec, extra, held, leaf, meanwhile=()):
        for step in range(4):
            args = []
            for s in range(SETS):
                args += [held[2 * s], send_to(held[2 * s + 1], ROUTE_XY[s][step])]
            if step < 3:
                held = call(functools.partial(split_kernel, rec, step + 1), bits, args, pairs(rec, (4 >> step) + extra))
        size = sum(rec) * (1 if extra == 1 else 2)
        keep, send = call(leaf, bits, args, [shape(size, HALF)] * 2)
        total = keep + send_to(send, ROUTE_Z1)
        total = total + send_to(total, ROUTE_Z2)
        got, *meanwhile = lax.optimization_barrier((send_to(total, ROUTE_Z3), *meanwhile))
        total = total + got
        return (total, send_to(total, ROUTE_C), *meanwhile)

    shared = ((1, 8), (0, 8), (0, 9), (1, 9))
    gram_parts = start(GRAM, (10, 10), shared, (end_grams_kernel, patch_grams_kernel), (bits, bits))
    got0, later0 = lax.optimization_barrier((gram_parts[1], bits))
    got1, later1 = lax.optimization_barrier((gram_parts[3], bits))
    gram_parts = [gram_parts[0], got0, gram_parts[2], got1]
    tile_parts = start(TILE, (8, 9), ((1, 8),), (end_tiles_kernel, patch_tiles_kernel), (later0, later1))
    held = begin(GRAM, (10, 10), shared, gram_parts)
    grams = chain(GRAM, 4, held, gram_leaf_kernel)
    held = begin(TILE, (8, 9), ((1, 8),), tile_parts)
    inverses = call(
        functools.partial(inverse_kernel, count),
        bits,
        grams,
        [shape(MID, MID)] * 2,
        room=16,
    )
    *tiles, left, right = chain(TILE, 1, held, tile_leaf_kernel, inverses)
    mine = call(
        functools.partial(apply_kernel, count),
        bits,
        (left, right, *tiles),
        [jax.ShapeDtypeStruct((HALF, MID), BF16)],
    )
    other = send_to(mine, ROUTE_Z1)
    tile, last = jnp.where(odd == 0, mine, other), jnp.where(odd == 0, other, mine)
    tiles = jnp.broadcast_to(tile[None], (16, HALF, MID))
    tiles = lax.all_to_all(tiles, ("y", "x_lo", "x_hi"), 0, 0)
    pieces = (tiles, send_to(tiles, ROUTE_C), last, send_to(last, ROUTE_C))
    outs = [
        jax.ShapeDtypeStruct((wide, middle), BF16),
        jax.ShapeDtypeStruct((9 * middle, middle), BF16),
        jax.ShapeDtypeStruct((middle, wide), BF16),
    ]
    return call(place_kernel, bits, pieces, outs)


def solution(mesh):
    mesh = Mesh(mesh.devices.reshape(SIZES), AXES)
    placed = P(AXES, None, None, None)
    return jax.shard_map(on_device, mesh=mesh, in_specs=(placed,) * 6, out_specs=(P(), P(), P()), check_vma=False)
```

```python
import functools

import jax
import jax.numpy as jnp
from jax import lax
from jax.experimental import pallas as pl
from jax.experimental.pallas import tpu as pltpu
from jax.sharding import Mesh
from jax.sharding import PartitionSpec as P

NS_ITERS = 6
DAMPING = 0.1
MID = 256
HALF = 128
SETS = 2
F32 = jnp.float32
BF16 = jnp.bfloat16

GRAM = (72, 64)
TILE = (128, 128)
ORDER = (((3, 2, 1, 0), (1, 0, 3, 2)), ((2, 3, 0, 1), (0, 1, 2, 3)))
def slot(order, q):
    return sum(((q >> order[k]) & 1) << (3 - k) for k in range(4))


def dot_t(a, b):
    return lax.dot_general(a, b, (((0,), (0,)), ((), ())), preferred_element_type=F32)


def iotas(n=HALF):
    return lax.broadcasted_iota(jnp.int32, (n, n), 0), lax.broadcasted_iota(jnp.int32, (n, n), 1)


def put(side, keep, send, at, low, high):
    n = low.shape[0]
    keep[at : at + n, :] = jnp.where(side, high, low)
    send[at : at + n, :] = jnp.where(side, low, high)


def put_gram(side, keep, send, many, i, gram):
    r, c = iotas()
    a, b, d = gram[:HALF, :HALF], gram[:HALF, HALF:], gram[HALF:, HALF:]
    fold = jnp.where(r <= c, a, d)
    for s in range(SETS):
        at = many * sum(GRAM[:s]) + i * GRAM[s]
        put(side, keep, send, at, fold[64 * s : 64 * s + 64], b[64 * s : 64 * s + 64])
    diag = jnp.broadcast_to(jnp.sum(jnp.where(r == c, d, 0.0), axis=0, keepdims=True), (8, HALF))
    put(side, keep, send, i * GRAM[0] + 64, diag, diag)


def put_tile(side, keep, send, many, i, tile):
    for s in range(SETS):
        rows = tile[HALF * s : HALF * s + HALF]
        put(side, keep, send, many * sum(TILE[:s]) + i * TILE[s], rows[:, :HALF], rows[:, HALF:])


def columns(ref, k=0):
    h, w, n, _ = ref.shape
    return ref[:, :, :, MID * k : MID * k + MID].reshape(h * w * n, MID)


def end_grams_kernel(bits, aw, an, g1, g3, keep, send):
    side = bits[0] == 1
    blocks = [(aw, k) for k in range(4)] + [(g3, k) for k in range(4)] + [(g1, 0), (an, 0)]
    for i, block in enumerate(blocks):
        own = columns(*block)
        put_gram(side, keep, send, 10, i, dot_t(own, own))


def end_tiles_kernel(bits, aw, an, g1, g3, keep, send):
    side = bits[0] == 1
    first_out, third_in = columns(g1), columns(an)
    for q in range(8):
        tile = dot_t(columns(aw, q), first_out) if q < 4 else dot_t(third_in, columns(g3, q - 4))
        put_tile(side, keep, send, 8, q, tile)


def widen(value, before):
    h, w, n, c = value.shape
    blank = lambda k: [jnp.zeros((h, k, n, c), BF16)] if k else []
    return jnp.concatenate(blank(before) + [value] + blank(16 - w - before), axis=1).reshape(h * 16 * n, c)


def shift(am, lines):
    h, w, n, c = am.shape
    step = 16 * n
    for dx, moved in enumerate((widen(am[:, : w - 1], 1), widen(am, 0), widen(am[:, 1:], 0))):
        lines[dx, :step, :] = jnp.zeros((step, c), BF16)
        lines[dx, step : step + h * step, :] = moved
        lines[dx, step + h * step :, :] = jnp.zeros((step, c), BF16)
    return step


def patch_grams_kernel(bits, both, keep, send, lines):
    side = bits[0] == 1
    am, g2 = both[: both.shape[0] // 2], both[both.shape[0] // 2 :]
    step = shift(am, lines)
    second_out = columns(g2)
    put_gram(side, keep, send, 10, 9, dot_t(second_out, second_out))
    end = step * (am.shape[0] + 1)
    for dx in range(3):
        cuts = (step, 2 * step), (2 * step, end - step), (end - step, end)
        top, inner, bottom = (dot_t(lines[dx, lo:hi, :], lines[dx, lo:hi, :]) for lo, hi in cuts)
        upper = inner + top
        put_gram(side, keep, send, 10, dx, upper)
        put_gram(side, keep, send, 10, 3 + dx, upper + bottom)
        put_gram(side, keep, send, 10, 6 + dx, inner + bottom)


def patch_tiles_kernel(bits, both, keep, send, lines):
    side = bits[0] == 1
    am, g2 = both[: both.shape[0] // 2], both[both.shape[0] // 2 :]
    step = shift(am, lines)
    second_out = widen(g2, 0)
    span = second_out.shape[0]
    for q in range(9):
        at = step * (q // 3)
        put_tile(side, keep, send, 9, q, dot_t(lines[q % 3, at : at + span, :], second_out))


def first_split_kernel(rec, many, extra, bits, keep0, got0, keep1, got1, *outs):
    for core in range(2):

        @pl.when(bits[0] == core)
        def _(core=core):
            first_split(ORDER[core], rec, many, extra, bits, ((keep0, got0), (keep1, got1)), outs)


def first_split(orders, rec, many, extra, bits, parts, outs):
    for s in range(SETS):
        keep, send = outs[2 * s], outs[2 * s + 1]
        lead = orders[s][0]
        side = bits[1 + lead] == 1
        n = rec[s]

        def summed(part, i):
            mine, got = parts[part]
            at = many[part] * sum(rec[:s]) + i * n
            return mine[at : at + n, :] + got[at : at + n, :]

        for q in range(16):
            if (q >> lead) & 1:
                continue
            other = q | 1 << lead
            put(side, keep, send, slot(orders[s], q) * n, summed(q // 8, q % 8), summed(other // 8, other % 8))
        for i, (part, j) in enumerate(extra):
            value = summed(part, j)
            keep[(8 + i) * n : (9 + i) * n, :] = value
            send[(8 + i) * n : (9 + i) * n, :] = value


def split_kernel(rows, s, step, bits, mine, got, keep, send):
    size = (8 >> step) * rows
    bit = bits[9 + 4 * s + step]
    here = pl.ds(pl.multiple_of(bit * size, 8), size)
    there = pl.ds(pl.multiple_of((1 - bit) * size, 8), size)
    keep[:size, :] = mine[here, :] + got[here, :]
    send[:size, :] = mine[there, :] + got[there, :]
    value = mine[2 * size :, :] + got[2 * size :, :]
    keep[size:, :] = value
    send[size:, :] = value


def gram_leaf_kernel(bits, mine0, got0, mine1, got1, keep, send):
    kind = bits[6]
    side = bits[5] == 1
    for s, (mine, got) in enumerate(((mine0, got0), (mine1, got1))):
        n = GRAM[s]
        at = 2 * sum(GRAM[:s])
        put(side, keep, send, at, mine[:n, :] + got[:n, :], mine[n : 2 * n, :] + got[n : 2 * n, :])
        chosen = pl.ds(pl.multiple_of((2 + kind) * n, 8), n)
        put(side, keep, send, at + n, mine[chosen, :] + got[chosen, :], mine[4 * n :, :] + got[4 * n :, :])


def tile_leaf_kernel(bits, mine0, got0, mine1, got1, keep, send):
    side = bits[5] == 1
    for s, (mine, got) in enumerate(((mine0, got0), (mine1, got1))):
        n = TILE[s]
        put(side, keep, send, n * s, mine[:n, :] + got[:n, :], mine[n:, :] + got[n:, :])


def halves(x):
    high = x.astype(BF16)
    return high, (x - high.astype(F32)).astype(BF16)


def mm3(a, b):
    (ah, al), (bh, bl) = halves(a), halves(b)
    return jnp.dot(ah, bh, preferred_element_type=F32) + (
        jnp.dot(ah, bl, preferred_element_type=F32) + jnp.dot(al, bh, preferred_element_type=F32)
    )


def mm(a, b):
    return jnp.dot(a, b, precision=lax.Precision.HIGHEST, preferred_element_type=F32)


def unfold(fold, b, diag):
    r, c = iotas()
    turned = fold.T
    a = jnp.where(r <= c, fold, turned)
    d = jnp.where(r > c, fold, jnp.where(r < c, turned, jnp.broadcast_to(diag, fold.shape)))
    top = jnp.concatenate([a, b], axis=1)
    return jnp.concatenate([top, jnp.concatenate([b.T, d], axis=1)], axis=0)


def residual(gram, count):
    r, c = iotas(MID)
    matrix = gram / count
    level = jnp.sum(jnp.where(r == c, matrix, 0.0)) / MID
    matrix = matrix + jnp.where(r == c, DAMPING * level, 0.0)
    bound = jnp.max(jnp.sum(jnp.abs(matrix), axis=0, keepdims=True))
    return jnp.where(r == c, 1.0, 0.0) - matrix / bound, bound


def inverse_kernel(count, bits, mine, mate, left_out, right_out):
    side = bits[0] == 1
    low = jnp.where(side, mate[...], mine[...])
    high = jnp.where(side, mine[...], mate[...])

    def gram(i):
        starts = [2 * sum(GRAM[:s]) + i * GRAM[s] for s in range(SETS)]
        fold, b = (jnp.concatenate([part[at : at + 64] for at in starts], axis=0) for part in (low, high))
        return unfold(fold, b, low[starts[0] + 64 : starts[0] + 65])

    r, c = iotas(MID)
    own, shared = residual(gram(0), count), residual(gram(1), count)
    powers = [own[0], shared[0]]
    sums = [jnp.where(r == c, 1.0, 0.0) + e for e in powers]
    for step in range(1, NS_ITERS):
        times = mm if step < 3 else mm3
        powers = [times(e, e) for e in powers]
        sums = [x + mm3(x, e) for x, e in zip(sums, powers)]
    own, shared = sums[0] / own[1], sums[1] / shared[1]
    third = bits[7] == 1
    left_out[...] = jnp.where(third, shared, own)
    right_out[...] = jnp.where(third, own, shared)


def apply_kernel(count, bits, left, right, mine, mate, out):
    side = bits[0] == 1
    low = jnp.where(side, mate[...], mine[...])
    high = jnp.where(side, mine[...], mate[...])
    tile = jnp.concatenate([low, high], axis=1) / count
    rows = left[pl.ds(pl.multiple_of(bits[0] * HALF, HALF), HALF), :]
    out[...] = mm(mm(rows, tile), right[...]).astype(BF16)


def place_kernel(bits, mine, mate, last, last_mate, out1, out2, out3):
    side = bits[0] == 1
    for half in range(2):
        swap = side if half == 0 else jnp.logical_not(side)
        at = half * HALF
        for j in range(16):
            value = jnp.where(swap, mate[j], mine[j])
            q = tile_of(j // 4, j % 2 * 2 + j // 2 % 2)
            if q < 4:
                out1[q * MID + at : q * MID + at + HALF, :] = value
            elif q < 8:
                out3[at : at + HALF, (q - 4) * MID : (q - 3) * MID] = value
            else:
                out2[(q - 8) * MID + at : (q - 8) * MID + at + HALF, :] = value
        out2[8 * MID + at : 8 * MID + at + HALF, :] = jnp.where(swap, last_mate[...], last[...])


VMEM = pl.BlockSpec(memory_space=pltpu.VMEM)
SMEM = pl.BlockSpec(memory_space=pltpu.SMEM)


def scratch_arrays(scratch):
    return [jax.ShapeDtypeStruct(a.shape, a.dtype) for a in scratch]


def call(kernel, bits, args, outs, scratch=(), flops=0, room=4):
    size = sum(a.size * a.dtype.itemsize for a in args) + sum(o.size * o.dtype.itemsize for o in outs)
    held = sum(a.size * a.dtype.itemsize for a in scratch_arrays(scratch))
    many = len(outs) > 1
    return pl.pallas_call(
        kernel,
        out_shape=tuple(outs) if many else outs[0],
        in_specs=[SMEM] + [VMEM] * len(args),
        out_specs=tuple([VMEM] * len(outs)) if many else VMEM,
        scratch_shapes=list(scratch),
        compiler_params=pltpu.CompilerParams(vmem_limit_bytes=size * 5 // 4 + held + room * 2**20),
        cost_estimate=pl.CostEstimate(flops=flops or 7 * 10**8, bytes_accessed=size if flops else 1024, transcendentals=0),
    )(bits, *args)


AXES = ("y", "x_lo", "z", "x_hi", "core")
SIZES = (4, 2, 8, 2, 2)


def place_of(device):
    rep, own = divmod(device, 32)
    return rep // 2, (own // 2) % 2 * 2 + rep % 2, own // 4, own % 2


def device_of(y, x, z, c):
    return (y * 2 + x % 2) * 32 + z * 4 + x // 2 * 2 + c


def route(move):
    return [(d, device_of(*move(*place_of(d)))) for d in range(256)]


ROUTE_C = route(lambda y, x, z, c: (y, x, z, 1 - c))
MOVE = {
    3: lambda y, x, z, c: (y, x ^ 1, z, c),
    2: lambda y, x, z, c: (y, 3 - x, z, c),
    1: lambda y, x, z, c: (y ^ 1, x, z, c),
    0: lambda y, x, z, c: (3 - y, x, z, c),
}
ROUTE_XY = [
    [route(lambda y, x, z, c: MOVE[ORDER[c][s][step]](y, x, z, c)) for step in range(4)] for s in range(SETS)
]
ROUTE_Z1 = route(lambda y, x, z, c: (y, x, z ^ 1, c))
ROUTE_Z2 = route(lambda y, x, z, c: (y, x, (z - 1 + 2 * (z % 2)) % 8, c))
ROUTE_Z3 = route(lambda y, x, z, c: (y, x, (3, 6, 5, 0, 7, 2, 1, 4)[z], c))


def tile_of(y, x):
    return ((x ^ (x >> 1)) & 1) * 8 + (x >> 1) * 4 + ((y ^ (y >> 1)) & 1) * 2 + (y >> 1)


def send_to(value, way):
    return lax.ppermute(value, AXES, way)


def on_device(act_wide, act_middle, act_narrow, grad_first, grad_second, grad_third):
    images, height, width, wide = act_wide.shape
    middle = act_middle.shape[3]
    count = float(images * height * width * 256)
    y, z, core = lax.axis_index("y"), lax.axis_index("z"), lax.axis_index("core")
    x = lax.axis_index("x_hi") * 2 + lax.axis_index("x_lo")
    q = tile_of(y, x)
    own = [(q >> i) & 1 for i in range(4)]
    turns = [jnp.where(core == 1, own[ORDER[1][s][k]], own[ORDER[0][s][k]]) for s in range(SETS) for k in range(4)]
    odd = ((z + 1) >> 1) & 1
    kind = jnp.where(q < 4, 0, jnp.where(q < 8, 1, 2))
    third = jnp.where((kind == 1) & (odd == 0), 1, 0)
    bits = jnp.stack([core, *own, odd, kind, third, q, *turns]).astype(jnp.int32)

    def shape(*dims):
        return jax.ShapeDtypeStruct(dims, F32)

    maps = [pltpu.VMEM((3, (height + 2) * 16 * images, middle), BF16)]
    ends = [a.transpose(1, 2, 0, 3) for a in (act_wide, act_narrow, grad_first, grad_third)]
    patches = [jnp.concatenate([a.transpose(1, 2, 0, 3) for a in (act_middle, grad_second)], axis=0)]

    def pairs(rec, records):
        return [shape(records * rec[s], HALF) for s in range(SETS) for _ in range(2)]

    def start(rec, many, extra, kernels, bits):
        parts = []
        for part, args, scratch in ((1, patches, maps), (0, ends, ())):
            outs = [shape(many[part] * sum(rec), HALF)] * 2
            keep, send = call(kernels[part], bits[part], args, outs, scratch, 2 * many[part] * 900 * 65536)
            parts = [keep, send_to(send, ROUTE_C)] + parts
        return parts

    def begin(rec, many, extra, parts):
        outs = pairs(rec, 8 + len(extra))
        return call(functools.partial(first_split_kernel, rec, many, extra), bits, parts, outs)

    def chain(rec, extra, held, leaf, meanwhile=()):
        for step in range(4):
            args = []
            for s in range(SETS):
                args += [held[2 * s], send_to(held[2 * s + 1], ROUTE_XY[s][step])]
            if step < 3:
                outs = pairs(rec, (4 >> step) + extra)
                held = []
                for s in range(SETS):
                    split = functools.partial(split_kernel, rec[s], s, step + 1)
                    held += call(split, bits, args[2 * s : 2 * s + 2], outs[2 * s : 2 * s + 2])
        size = sum(rec) * (1 if extra == 1 else 2)
        keep, send = call(leaf, bits, args, [shape(size, HALF)] * 2)
        total = keep + send_to(send, ROUTE_Z1)
        total = total + send_to(total, ROUTE_Z2)
        got, *meanwhile = lax.optimization_barrier((send_to(total, ROUTE_Z3), *meanwhile))
        total = total + got
        return (total, send_to(total, ROUTE_C), *meanwhile)

    shared = ((1, 8), (0, 8), (0, 9), (1, 9))
    gram_parts = start(GRAM, (10, 10), shared, (end_grams_kernel, patch_grams_kernel), (bits, bits))
    got0, later0 = lax.optimization_barrier((gram_parts[1], bits))
    got1, later1 = lax.optimization_barrier((gram_parts[3], bits))
    gram_parts = [gram_parts[0], got0, gram_parts[2], got1]
    tile_parts = start(TILE, (8, 9), ((1, 8),), (end_tiles_kernel, patch_tiles_kernel), (later0, later1))
    held = begin(GRAM, (10, 10), shared, gram_parts)
    grams = chain(GRAM, 4, held, gram_leaf_kernel)
    held = begin(TILE, (8, 9), ((1, 8),), tile_parts)
    inverses = call(
        functools.partial(inverse_kernel, count),
        bits,
        grams,
        [shape(MID, MID)] * 2,
        room=16,
    )
    *tiles, left, right = chain(TILE, 1, held, tile_leaf_kernel, inverses)
    mine = call(
        functools.partial(apply_kernel, count),
        bits,
        (left, right, *tiles),
        [jax.ShapeDtypeStruct((HALF, MID), BF16)],
    )
    other = send_to(mine, ROUTE_Z1)
    tile, last = jnp.where(odd == 0, mine, other), jnp.where(odd == 0, other, mine)
    tiles = jnp.broadcast_to(tile[None], (16, HALF, MID))
    tiles = lax.all_to_all(tiles, ("y", "x_lo", "x_hi"), 0, 0)
    pieces = (tiles, send_to(tiles, ROUTE_C), last, send_to(last, ROUTE_C))
    outs = [
        jax.ShapeDtypeStruct((wide, middle), BF16),
        jax.ShapeDtypeStruct((9 * middle, middle), BF16),
        jax.ShapeDtypeStruct((middle, wide), BF16),
    ]
    return call(place_kernel, bits, pieces, outs)


def solution(mesh):
    mesh = Mesh(mesh.devices.reshape(SIZES), AXES)
    placed = P(AXES, None, None, None)
    return jax.shard_map(on_device, mesh=mesh, in_specs=(placed,) * 6, out_specs=(P(), P(), P()), check_vma=False)
```

```python
import functools

import jax
import jax.numpy as jnp
from jax import lax
from jax.experimental import pallas as pl
from jax.experimental.pallas import tpu as pltpu
from jax.sharding import Mesh
from jax.sharding import PartitionSpec as P

NS_ITERS = 6
DAMPING = 0.1
MID = 256
HALF = 128
SETS = 2
F32 = jnp.float32
BF16 = jnp.bfloat16

GRAM = (72, 64)
TILE = (128, 128)
ORDER = (((3, 2, 1, 0), (1, 0, 3, 2)), ((2, 3, 0, 1), (0, 1, 2, 3)))
def slot(order, q):
    return sum(((q >> order[k]) & 1) << (3 - k) for k in range(4))


def dot_t(a, b):
    return lax.dot_general(a, b, (((0,), (0,)), ((), ())), preferred_element_type=F32)


def iotas(n=HALF):
    return lax.broadcasted_iota(jnp.int32, (n, n), 0), lax.broadcasted_iota(jnp.int32, (n, n), 1)


def put(side, keep, send, at, low, high):
    n = low.shape[0]
    keep[at : at + n, :] = jnp.where(side, high, low)
    send[at : at + n, :] = jnp.where(side, low, high)


def put_gram(side, keep, send, many, i, gram):
    r, c = iotas()
    a, b, d = gram[:HALF, :HALF], gram[:HALF, HALF:], gram[HALF:, HALF:]
    fold = jnp.where(r <= c, a, d)
    for s in range(SETS):
        at = many * sum(GRAM[:s]) + i * GRAM[s]
        put(side, keep, send, at, fold[64 * s : 64 * s + 64], b[64 * s : 64 * s + 64])
    diag = jnp.broadcast_to(jnp.sum(jnp.where(r == c, d, 0.0), axis=0, keepdims=True), (8, HALF))
    put(side, keep, send, i * GRAM[0] + 64, diag, diag)


def put_tile(side, keep, send, many, i, tile):
    for s in range(SETS):
        rows = tile[HALF * s : HALF * s + HALF]
        put(side, keep, send, many * sum(TILE[:s]) + i * TILE[s], rows[:, :HALF], rows[:, HALF:])


def columns(ref, k=0):
    h, w, n, _ = ref.shape
    return ref[:, :, :, MID * k : MID * k + MID].reshape(h * w * n, MID)


def end_grams_kernel(bits, aw, an, g1, g3, keep, send):
    side = bits[0] == 1
    blocks = [(aw, k) for k in range(4)] + [(g3, k) for k in range(4)] + [(g1, 0), (an, 0)]
    for i, block in enumerate(blocks):
        own = columns(*block)
        put_gram(side, keep, send, 10, i, dot_t(own, own))


def end_tiles_kernel(bits, aw, an, g1, g3, keep, send):
    side = bits[0] == 1
    first_out, third_in = columns(g1), columns(an)
    for q in range(8):
        tile = dot_t(columns(aw, q), first_out) if q < 4 else dot_t(third_in, columns(g3, q - 4))
        put_tile(side, keep, send, 8, q, tile)


def widen(value, before):
    h, w, n, c = value.shape
    blank = lambda k: [jnp.zeros((h, k, n, c), BF16)] if k else []
    return jnp.concatenate(blank(before) + [value] + blank(16 - w - before), axis=1).reshape(h * 16 * n, c)


def shift(am, lines):
    h, w, n, c = am.shape
    step = 16 * n
    for dx, moved in enumerate((widen(am[:, : w - 1], 1), widen(am, 0), widen(am[:, 1:], 0))):
        lines[dx, :step, :] = jnp.zeros((step, c), BF16)
        lines[dx, step : step + h * step, :] = moved
        lines[dx, step + h * step :, :] = jnp.zeros((step, c), BF16)
    return step


def patch_grams_kernel(bits, both, keep, send, lines):
    side = bits[0] == 1
    am, g2 = both[: both.shape[0] // 2], both[both.shape[0] // 2 :]
    step = shift(am, lines)
    second_out = columns(g2)
    put_gram(side, keep, send, 10, 9, dot_t(second_out, second_out))
    end = step * (am.shape[0] + 1)
    for dx in range(3):
        cuts = (step, 2 * step), (2 * step, end - step), (end - step, end)
        top, inner, bottom = (dot_t(lines[dx, lo:hi, :], lines[dx, lo:hi, :]) for lo, hi in cuts)
        upper = inner + top
        put_gram(side, keep, send, 10, dx, upper)
        put_gram(side, keep, send, 10, 3 + dx, upper + bottom)
        put_gram(side, keep, send, 10, 6 + dx, inner + bottom)


def patch_tiles_kernel(bits, both, keep, send, lines):
    side = bits[0] == 1
    am, g2 = both[: both.shape[0] // 2], both[both.shape[0] // 2 :]
    step = shift(am, lines)
    second_out = widen(g2, 0)
    span = second_out.shape[0]
    for q in range(9):
        at = step * (q // 3)
        put_tile(side, keep, send, 9, q, dot_t(lines[q % 3, at : at + span, :], second_out))


def first_split_kernel(rec, many, extra, bits, keep0, got0, keep1, got1, *outs):
    for core in range(2):

        @pl.when(bits[0] == core)
        def _(core=core):
            first_split(ORDER[core], rec, many, extra, bits, ((keep0, got0), (keep1, got1)), outs)


def first_split(orders, rec, many, extra, bits, parts, outs):
    for s in range(SETS):
        keep, send = outs[2 * s], outs[2 * s + 1]
        lead = orders[s][0]
        side = bits[1 + lead] == 1
        n = rec[s]

        def summed(part, i):
            mine, got = parts[part]
            at = many[part] * sum(rec[:s]) + i * n
            return mine[at : at + n, :] + got[at : at + n, :]

        for q in range(16):
            if (q >> lead) & 1:
                continue
            other = q | 1 << lead
            put(side, keep, send, slot(orders[s], q) * n, summed(q // 8, q % 8), summed(other // 8, other % 8))
        for i, (part, j) in enumerate(extra):
            value = summed(part, j)
            keep[(8 + i) * n : (9 + i) * n, :] = value
            send[(8 + i) * n : (9 + i) * n, :] = value


def split_kernel(rows, s, step, bits, mine, got, keep, send):
    size = (8 >> step) * rows
    bit = bits[9 + 4 * s + step]
    here = pl.ds(pl.multiple_of(bit * size, 8), size)
    there = pl.ds(pl.multiple_of((1 - bit) * size, 8), size)
    keep[:size, :] = mine[here, :] + got[here, :]
    send[:size, :] = mine[there, :] + got[there, :]
    value = mine[2 * size :, :] + got[2 * size :, :]
    keep[size:, :] = value
    send[size:, :] = value


def gram_leaf_kernel(bits, mine0, got0, mine1, got1, keep, send):
    kind = bits[6]
    side = bits[5] == 1
    for s, (mine, got) in enumerate(((mine0, got0), (mine1, got1))):
        n = GRAM[s]
        at = 2 * sum(GRAM[:s])
        put(side, keep, send, at, mine[:n, :] + got[:n, :], mine[n : 2 * n, :] + got[n : 2 * n, :])
        chosen = pl.ds(pl.multiple_of((2 + kind) * n, 8), n)
        put(side, keep, send, at + n, mine[chosen, :] + got[chosen, :], mine[4 * n :, :] + got[4 * n :, :])


def tile_leaf_kernel(bits, mine0, got0, mine1, got1, keep, send):
    side = bits[5] == 1
    for s, (mine, got) in enumerate(((mine0, got0), (mine1, got1))):
        n = TILE[s]
        put(side, keep, send, n * s, mine[:n, :] + got[:n, :], mine[n:, :] + got[n:, :])


def halves(x):
    high = x.astype(BF16)
    return high, (x - high.astype(F32)).astype(BF16)


def mm3(a, b):
    (ah, al), (bh, bl) = halves(a), halves(b)
    return jnp.dot(ah, bh, preferred_element_type=F32) + (
        jnp.dot(ah, bl, preferred_element_type=F32) + jnp.dot(al, bh, preferred_element_type=F32)
    )


def mm(a, b):
    return jnp.dot(a, b, precision=lax.Precision.HIGHEST, preferred_element_type=F32)


def unfold(fold, b, diag):
    r, c = iotas()
    turned = fold.T
    a = jnp.where(r <= c, fold, turned)
    d = jnp.where(r > c, fold, jnp.where(r < c, turned, jnp.broadcast_to(diag, fold.shape)))
    top = jnp.concatenate([a, b], axis=1)
    return jnp.concatenate([top, jnp.concatenate([b.T, d], axis=1)], axis=0)


def residual(gram, count):
    r, c = iotas(MID)
    matrix = gram / count
    level = jnp.sum(jnp.where(r == c, matrix, 0.0)) / MID
    matrix = matrix + jnp.where(r == c, DAMPING * level, 0.0)
    bound = jnp.max(jnp.sum(jnp.abs(matrix), axis=0, keepdims=True))
    return jnp.where(r == c, 1.0, 0.0) - matrix / bound, bound


def inverse_kernel(count, bits, mine, mate, left_out, right_out):
    side = bits[0] == 1
    low = jnp.where(side, mate[...], mine[...])
    high = jnp.where(side, mine[...], mate[...])

    def gram(i):
        starts = [2 * sum(GRAM[:s]) + i * GRAM[s] for s in range(SETS)]
        fold, b = (jnp.concatenate([part[at : at + 64] for at in starts], axis=0) for part in (low, high))
        return unfold(fold, b, low[starts[0] + 64 : starts[0] + 65])

    r, c = iotas(MID)
    own, shared = residual(gram(0), count), residual(gram(1), count)
    powers = [own[0], shared[0]]
    sums = [jnp.where(r == c, 1.0, 0.0) + e for e in powers]
    for step in range(1, NS_ITERS):
        times = mm if step < 3 else mm3
        powers = [times(e, e) for e in powers]
        sums = [x + mm3(x, e) for x, e in zip(sums, powers)]
    own, shared = sums[0] / own[1], sums[1] / shared[1]
    third = bits[7] == 1
    left_out[...] = jnp.where(third, shared, own)
    right_out[...] = jnp.where(third, own, shared)


def apply_kernel(count, bits, left, right, mine, mate, out):
    side = bits[0] == 1
    low = jnp.where(side, mate[...], mine[...])
    high = jnp.where(side, mine[...], mate[...])
    tile = jnp.concatenate([low, high], axis=1) / count
    rows = left[pl.ds(pl.multiple_of(bits[0] * HALF, HALF), HALF), :]
    out[...] = mm(mm(rows, tile), right[...]).astype(BF16)


def place_kernel(bits, mine, mate, last, last_mate, out1, out2, out3):
    side = bits[0] == 1
    for half in range(2):
        swap = side if half == 0 else jnp.logical_not(side)
        at = half * HALF
        for j in range(16):
            value = jnp.where(swap, mate[j], mine[j])
            q = tile_of(j // 4, j % 2 * 2 + j // 2 % 2)
            if q < 4:
                out1[q * MID + at : q * MID + at + HALF, :] = value
            elif q < 8:
                out3[at : at + HALF, (q - 4) * MID : (q - 3) * MID] = value
            else:
                out2[(q - 8) * MID + at : (q - 8) * MID + at + HALF, :] = value
        out2[8 * MID + at : 8 * MID + at + HALF, :] = jnp.where(swap, last_mate[...], last[...])


VMEM = pl.BlockSpec(memory_space=pltpu.VMEM)
SMEM = pl.BlockSpec(memory_space=pltpu.SMEM)


def scratch_arrays(scratch):
    return [jax.ShapeDtypeStruct(a.shape, a.dtype) for a in scratch]


def call(kernel, bits, args, outs, scratch=(), flops=0, room=4):
    size = sum(a.size * a.dtype.itemsize for a in args) + sum(o.size * o.dtype.itemsize for o in outs)
    held = sum(a.size * a.dtype.itemsize for a in scratch_arrays(scratch))
    many = len(outs) > 1
    return pl.pallas_call(
        kernel,
        out_shape=tuple(outs) if many else outs[0],
        in_specs=[SMEM] + [VMEM] * len(args),
        out_specs=tuple([VMEM] * len(outs)) if many else VMEM,
        scratch_shapes=list(scratch),
        compiler_params=pltpu.CompilerParams(vmem_limit_bytes=size * 5 // 4 + held + room * 2**20),
        cost_estimate=pl.CostEstimate(flops=flops or 10**9, bytes_accessed=size if flops else 1024, transcendentals=0),
    )(bits, *args)


AXES = ("y", "x_lo", "z", "x_hi", "core")
SIZES = (4, 2, 8, 2, 2)


def place_of(device):
    rep, own = divmod(device, 32)
    return rep // 2, (own // 2) % 2 * 2 + rep % 2, own // 4, own % 2


def device_of(y, x, z, c):
    return (y * 2 + x % 2) * 32 + z * 4 + x // 2 * 2 + c


def route(move):
    return [(d, device_of(*move(*place_of(d)))) for d in range(256)]


ROUTE_C = route(lambda y, x, z, c: (y, x, z, 1 - c))
MOVE = {
    3: lambda y, x, z, c: (y, x ^ 1, z, c),
    2: lambda y, x, z, c: (y, 3 - x, z, c),
    1: lambda y, x, z, c: (y ^ 1, x, z, c),
    0: lambda y, x, z, c: (3 - y, x, z, c),
}
ROUTE_XY = [
    [route(lambda y, x, z, c: MOVE[ORDER[c][s][step]](y, x, z, c)) for step in range(4)] for s in range(SETS)
]
ROUTE_Z1 = route(lambda y, x, z, c: (y, x, z ^ 1, c))
ROUTE_Z2 = route(lambda y, x, z, c: (y, x, (z - 1 + 2 * (z % 2)) % 8, c))
ROUTE_Z3 = route(lambda y, x, z, c: (y, x, (3, 6, 5, 0, 7, 2, 1, 4)[z], c))


def tile_of(y, x):
    return ((x ^ (x >> 1)) & 1) * 8 + (x >> 1) * 4 + ((y ^ (y >> 1)) & 1) * 2 + (y >> 1)


def send_to(value, way):
    return lax.ppermute(value, AXES, way)


def on_device(act_wide, act_middle, act_narrow, grad_first, grad_second, grad_third):
    images, height, width, wide = act_wide.shape
    middle = act_middle.shape[3]
    count = float(images * height * width * 256)
    y, z, core = lax.axis_index("y"), lax.axis_index("z"), lax.axis_index("core")
    x = lax.axis_index("x_hi") * 2 + lax.axis_index("x_lo")
    q = tile_of(y, x)
    own = [(q >> i) & 1 for i in range(4)]
    turns = [jnp.where(core == 1, own[ORDER[1][s][k]], own[ORDER[0][s][k]]) for s in range(SETS) for k in range(4)]
    odd = ((z + 1) >> 1) & 1
    kind = jnp.where(q < 4, 0, jnp.where(q < 8, 1, 2))
    third = jnp.where((kind == 1) & (odd == 0), 1, 0)
    bits = jnp.stack([core, *own, odd, kind, third, q, *turns]).astype(jnp.int32)

    def shape(*dims):
        return jax.ShapeDtypeStruct(dims, F32)

    maps = [pltpu.VMEM((3, (height + 2) * 16 * images, middle), BF16)]
    ends = [a.transpose(1, 2, 0, 3) for a in (act_wide, act_narrow, grad_first, grad_third)]
    patches = [jnp.concatenate([a.transpose(1, 2, 0, 3) for a in (act_middle, grad_second)], axis=0)]

    def pairs(rec, records):
        return [shape(records * rec[s], HALF) for s in range(SETS) for _ in range(2)]

    def start(rec, many, extra, kernels, bits):
        parts = []
        for part, args, scratch in ((1, patches, maps), (0, ends, ())):
            outs = [shape(many[part] * sum(rec), HALF)] * 2
            keep, send = call(kernels[part], bits[part], args, outs, scratch, 2 * many[part] * 900 * 65536)
            parts = [keep, send_to(send, ROUTE_C)] + parts
        return parts

    def begin(rec, many, extra, parts):
        outs = pairs(rec, 8 + len(extra))
        return call(functools.partial(first_split_kernel, rec, many, extra), bits, parts, outs)

    def chain(rec, extra, held, leaf, meanwhile=()):
        for step in range(4):
            args = []
            for s in range(SETS):
                args += [held[2 * s], send_to(held[2 * s + 1], ROUTE_XY[s][step])]
            if step < 3:
                outs = pairs(rec, (4 >> step) + extra)
                held = []
                for s in range(SETS):
                    split = functools.partial(split_kernel, rec[s], s, step + 1)
                    held += call(split, bits, args[2 * s : 2 * s + 2], outs[2 * s : 2 * s + 2])
        size = sum(rec) * (1 if extra == 1 else 2)
        keep, send = call(leaf, bits, args, [shape(size, HALF)] * 2)
        total = keep + send_to(send, ROUTE_Z1)
        total = total + send_to(total, ROUTE_Z2)
        got, *meanwhile = lax.optimization_barrier((send_to(total, ROUTE_Z3), *meanwhile))
        total = total + got
        return (total, send_to(total, ROUTE_C), *meanwhile)

    shared = ((1, 8), (0, 8), (0, 9), (1, 9))
    gram_parts = start(GRAM, (10, 10), shared, (end_grams_kernel, patch_grams_kernel), (bits, bits))
    got0, later0 = lax.optimization_barrier((gram_parts[1], bits))
    got1, later1 = lax.optimization_barrier((gram_parts[3], bits))
    gram_parts = [gram_parts[0], got0, gram_parts[2], got1]
    tile_parts = start(TILE, (8, 9), ((1, 8),), (end_tiles_kernel, patch_tiles_kernel), (later0, later1))
    held = begin(GRAM, (10, 10), shared, gram_parts)
    grams = chain(GRAM, 4, held, gram_leaf_kernel)
    held = begin(TILE, (8, 9), ((1, 8),), tile_parts)
    inverses = call(
        functools.partial(inverse_kernel, count),
        bits,
        grams,
        [shape(MID, MID)] * 2,
        room=16,
    )
    *tiles, left, right = chain(TILE, 1, held, tile_leaf_kernel, inverses)
    mine = call(
        functools.partial(apply_kernel, count),
        bits,
        (left, right, *tiles),
        [jax.ShapeDtypeStruct((HALF, MID), BF16)],
    )
    other = send_to(mine, ROUTE_Z1)
    tile, last = jnp.where(odd == 0, mine, other), jnp.where(odd == 0, other, mine)
    tiles = jnp.broadcast_to(tile[None], (16, HALF, MID))
    tiles = lax.all_to_all(tiles, ("y", "x_lo", "x_hi"), 0, 0)
    pieces = (tiles, send_to(tiles, ROUTE_C), last, send_to(last, ROUTE_C))
    outs = [
        jax.ShapeDtypeStruct((wide, middle), BF16),
        jax.ShapeDtypeStruct((9 * middle, middle), BF16),
        jax.ShapeDtypeStruct((middle, wide), BF16),
    ]
    return call(place_kernel, bits, pieces, outs)


def solution(mesh):
    mesh = Mesh(mesh.devices.reshape(SIZES), AXES)
    placed = P(AXES, None, None, None)
    return jax.shard_map(on_device, mesh=mesh, in_specs=(placed,) * 6, out_specs=(P(), P(), P()), check_vma=False)
```
